32 devices in a mesh: ty: 4 (over x, core), tx: 8 (over z, y).
Axes of the slice: x: 2, y: 2, z: 4, core: 2. Of those that a mesh axis runs over, the one named last changes fastest.
Arguments:
- roi_feat: bfloat16 [384, 14, 14, 256], P(('ty', 'tx')), may hold values from -6 to 6
- pre_one: bfloat16 [384, 14, 14, 256], P(('ty', 'tx')), may hold values from -6 to 6
- grad_two: bfloat16 [384, 14, 14, 256], P(('ty', 'tx')), may hold values from -6 to 6
- w_one: bfloat16 [3, 3, 256, 256], replicated, may hold values from -0.125 to 0.125
- w_two: bfloat16 [3, 3, 256, 256], replicated, may hold values from -0.125 to 0.125
- roi_rows: bfloat16 [384, 16, 14], P(('ty', 'tx')), may hold values from -1.5 to 1.5
- roi_cols: bfloat16 [384, 16, 14], P(('ty', 'tx')), may hold values from -1.5 to 1.5
- target_col: int32 [384, 1], P(('ty', 'tx')), may hold values from 0 to 7; in each aligned block of 12 rows (0 to 11, 12 to 23, ...) at most 3 rows name the same one
- off_row: int32 [384], P(('ty', 'tx')), may hold values from 0 to 15
- off_col: int32 [384], P(('ty', 'tx')), may hold values from 0 to 63
- fpn_input: bfloat16 [64, 512, 256], P('ty', 'tx'), may hold values from -6 to 6
- fpn_grad: bfloat16 [64, 512, 256], P('ty', 'tx'), may hold values from -6 to 6
- w_fpn: bfloat16 [3, 3, 256, 256], replicated, may hold values from -0.125 to 0.125
Outputs:
- grad_fpn_input: bfloat16 [64, 512, 256], P('ty', 'tx')
- grad_w_one: float32 [589824], P(('ty', 'tx'))
- grad_w_two: float32 [589824], P(('ty', 'tx'))
- grad_w_fpn: float32 [589824], P(('ty', 'tx'))
The draws below stay inside these ranges and needn't reach their ends.
Inputs may be any that keep to these rules, and one draw needn't show every extreme that they name: `target_col`: at most 3 regions of one device name the same column, and in every draw some device names some column exactly 3 times.
All inputs are finite; a program needn't handle non-finite values.
Results may differ from the reference program's by a relative error of at most 0.0075.
Values may be sent and summed in bfloat16 or wider, within the bound.
No kernel may reach another device: no remote copies, remote signals or barrier semaphores. Data moves between devices by JAX's collectives and lax.ppermute only.
A program may use at most 128 MiB of HBM per device.

```python
import math
import jax
import jax.numpy as jnp
import numpy as np
from jax import lax

C = 256
POOL = 14
BOX = 16
R_DEV = 12
TH = 16
TW = 64
CAP = 3
REGIONS = 384
H = 64
W = 512
N_TY = 4
N_TX = 8


def set_ends(entries, key, least, high):
    longest = entries.shape.index(max(entries.shape))
    spots = []
    for shift in (0, 1):
        where = [jax.random.randint(jax.random.fold_in(key, axis), (), 0, length) for axis, length in enumerate(entries.shape)]
        where[longest] = (where[longest] + shift) % entries.shape[longest]
        spots.append(tuple(where))
    return entries.at[spots[0]].set(least).at[spots[1]].set(high)


def spiked(drawn, rng, source, target, parts, factor):
    owner, partner = [(jnp.arange(drawn.shape[dim]) // (drawn.shape[dim] // parts)).reshape([-1 if axis == dim else 1 for axis in range(drawn.ndim)]) for dim in (source, target)]
    chosen = jax.random.permutation(rng, parts)[partner]
    strong = (owner == chosen) | (owner == (partner + parts // 2) % parts)
    return jnp.where(strong, factor * drawn, drawn)


def steps_of(stream_key, shape, shards, least, largest):
    loudness, own = 1.0, jax.random.fold_in(stream_key, 6)
    for dim, blocks in shards:
        heights = jnp.exp(jax.random.uniform(jax.random.fold_in(own, dim), (blocks,), jnp.float32, least / len(shards), largest / len(shards)))
        loudness = loudness * jnp.repeat(heights, shape[dim] // blocks).reshape([-1 if axis == dim else 1 for axis in range(len(shape))])
    return loudness


def deal_out(own_key, own, number, rows, number_of, top, reach, lean):
    order = jax.random.permutation(own_key, number_of)
    heavy_load, ordinary = portions_of(number_of, rows * top, reach, lean, True), portions_of(number_of, rows * top, reach, lean, False)
    places = jnp.arange(number_of)

    def named(tallies, offset_by):
        used = int((tallies > 0).sum())
        fixed = max(1, used // 4)
        shifted = fixed + (places - fixed + offset_by * (used - fixed)) % max(1, number_of - fixed)
        return jnp.zeros((number_of,), jnp.int32).at[order[jnp.where(places < fixed, places, shifted)]].set(jnp.asarray(tallies, jnp.int32))

    tallies = jnp.where(number % 4 == 0, named(heavy_load, number // 4), named(ordinary, number - number // 4 - 1))
    mixed = jax.random.permutation(jax.random.fold_in(own, 3), number_of)
    giver, receiver = mixed[0:number_of // 2 * 2:2], mixed[1:number_of // 2 * 2:2]
    room = jnp.minimum(tallies[giver] - 1, reach - tallies[receiver]) // 2
    room = jnp.where((giver == order[0]) | (receiver == order[0]) | (tallies[receiver] == 0), 0, jnp.maximum(room, 0))
    shifted = jax.random.randint(jax.random.fold_in(own, 4), (number_of // 2,), 0, 1 << 20) % (room + 1)
    tallies = tallies.at[giver].add(-shifted).at[receiver].add(shifted)
    labels = jnp.searchsorted(jnp.cumsum(tallies), jnp.arange(rows * top), side="right").astype(jnp.int32)
    table = labels.reshape(top, rows).T
    table = table[jax.random.permutation(jax.random.fold_in(own, 1), rows)]
    offset_by = jax.random.randint(jax.random.fold_in(own, 2), (rows, 1), 0, top)
    return jnp.take_along_axis(table, (jnp.arange(top)[None, :] + offset_by) % top, axis=1)


def portions_of(amount, total, bound, slope, full):
    loads = [(1 << 20) // math.isqrt(standing ** slope) + 1 for standing in range(1, amount + 1)]
    largest = bound if full else min(bound, max(-(-total // amount), total * loads[0] // sum(loads)))
    least = 1 if total - largest >= amount - 1 else 0
    holding, spare = [largest] + [least] * (amount - 1), total - largest - least * (amount - 1)
    while spare > 0:
        candidates = [i for i in range(1, amount) if holding[i] < largest] or [i for i in range(1, amount) if holding[i] < bound]
        whole, budget = sum([loads[i] for i in candidates]), spare
        for i in candidates:
            addition = min(bound - holding[i], max(1, budget * loads[i] // whole), spare)
            holding[i] = holding[i] + addition
            spare = spare - addition
    return np.array(holding)


def scatter_about(own_key, dims, spread, most, shards=(), kind=jnp.bfloat16):
    loudness = steps_of(own_key, dims, shards, -0.22, 0.18) if shards else 1.0
    entries = jax.random.normal(own_key, dims, jnp.float32) * spread * loudness
    return jnp.minimum(jnp.maximum(entries, -most), most).astype(kind)


def bell_draw_with(rng, dims, width, most, split, heavy, kind=jnp.bfloat16):
    drawn = width * jax.random.normal(rng, dims, jnp.float32)
    if split:
        drawn = drawn * steps_of(rng, dims, split, -0.22, 0.18)
    return jnp.clip(spiked(drawn, jax.random.fold_in(rng, 3), *heavy), -most, most).astype(kind)


def setup_inputs(seed: int = 0) -> dict:
    splits = jax.random.split(jax.random.key(seed), 14)
    roi_feat = scatter_about(splits[0], (REGIONS, POOL, POOL, C), 1.0, 6.0, ((0, 32),))
    pre_one = scatter_about(splits[1], (REGIONS, POOL, POOL, C), 1.0, 6.0, ((0, 32),))
    grad_two = bell_draw_with(splits[2], (REGIONS, POOL, POOL, C), 1.0, 6.0, ((0, 32),), (0, 3, 32, 2.75))
    w_one = scatter_about(splits[3], (3, 3, C, C), (9 * C) ** -0.5, 0.125)
    w_two = scatter_about(splits[4], (3, 3, C, C), (9 * C) ** -0.5, 0.125)
    roi_rows = scatter_about(splits[5], (REGIONS, BOX, POOL), POOL ** -0.5, 1.5, ((0, 32),))
    roi_cols = scatter_about(splits[6], (REGIONS, BOX, POOL), POOL ** -0.5, 1.5, ((0, 32),))
    target_col_keys = jax.random.split(jax.random.fold_in(splits[7], 1), REGIONS // R_DEV)
    target_col_turns = jax.random.permutation(jax.random.fold_in(splits[7], 3), REGIONS // R_DEV)
    target_col = jax.vmap(lambda own, number: deal_out(jax.random.fold_in(splits[7], 2), own, number, R_DEV, N_TX, 1, CAP, 2))(target_col_keys, target_col_turns).reshape((REGIONS, 1))
    off_row = set_ends(jax.random.randint(splits[8], (REGIONS,), 0, TH), jax.random.fold_in(splits[8], 1), 0, TH - 1).astype(jnp.int32)
    off_col = set_ends(jax.random.randint(splits[9], (REGIONS,), 0, TW), jax.random.fold_in(splits[9], 1), 0, TW - 1).astype(jnp.int32)
    fpn_input = scatter_about(splits[10], (H, W, C), 1.0, 6.0, ((0, 4), (1, 8)))
    fpn_grad = bell_draw_with(splits[11], (H, W, C), 1.0, 6.0, ((0, 4), (1, 8)), (0, 2, 4, 2.0))
    w_fpn = scatter_about(splits[12], (3, 3, C, C), (9 * C) ** -0.5, 0.125)
    return dict(roi_feat=roi_feat, pre_one=pre_one, grad_two=grad_two, w_one=w_one, w_two=w_two, roi_rows=roi_rows, roi_cols=roi_cols, target_col=target_col, off_row=off_row, off_col=off_col, fpn_input=fpn_input, fpn_grad=fpn_grad, w_fpn=w_fpn)


def window_patches(padded, row_count, col_count, flipped):
    pieces = []
    for row_step in range(3):
        for col_step in range(3):
            row_start = 2 - row_step if flipped else row_step
            col_start = 2 - col_step if flipped else col_step
            pieces.append(padded[..., row_start:row_start + row_count, col_start:col_start + col_count, :])
    return jnp.concatenate(pieces, axis=-1)


def flipped_weight(weight):
    channels = weight.shape[2]
    return jnp.transpose(weight, (0, 1, 3, 2)).reshape(9 * channels, channels)


def weight_term(gradient, inputs_patch):
    return lax.dot_general(gradient, inputs_patch, (((0,), (0,)), ((), ())), preferred_element_type=jnp.float32)


def region_windows(region_grad, row_weights, col_weights):
    highest = lax.Precision.HIGHEST
    partial_sum = jnp.einsum("nxj,nijc->nixc", col_weights.astype(jnp.float32), region_grad.astype(jnp.float32), precision=highest)
    return jnp.einsum("nyi,nixc->nyxc", row_weights.astype(jnp.float32), partial_sum, precision=highest).astype(jnp.bfloat16)


def reference(roi_feat, pre_one, grad_two, w_one, w_two, roi_rows, roi_cols, target_col, off_row, off_col, fpn_input, fpn_grad, w_fpn):
    region_pad = ((0, 0), (1, 1), (1, 1), (0, 0))
    block_count = REGIONS // R_DEV

    def head_block(totals, block):
        features_in, pre_act, upstream, row_weights, col_weights = block
        positions = R_DEV * POOL * POOL
        active = jnp.maximum(pre_act, 0).astype(jnp.bfloat16)
        back_two = jnp.dot(window_patches(jnp.pad(upstream, region_pad), POOL, POOL, True).reshape(positions, 9 * C), flipped_weight(w_two), preferred_element_type=jnp.float32)
        grad_one = jnp.where(pre_act.reshape(positions, C) > 0, back_two, 0.0).astype(jnp.bfloat16)
        term_two = weight_term(upstream.reshape(positions, C), window_patches(jnp.pad(active, region_pad), POOL, POOL, False).reshape(positions, 9 * C))
        term_one = weight_term(grad_one, window_patches(jnp.pad(features_in, region_pad), POOL, POOL, False).reshape(positions, 9 * C))
        region_grad = jnp.dot(window_patches(jnp.pad(grad_one.reshape(R_DEV, POOL, POOL, C), region_pad), POOL, POOL, True).reshape(positions, 9 * C), flipped_weight(w_one), preferred_element_type=jnp.float32).astype(jnp.bfloat16)
        windows = region_windows(region_grad.reshape(R_DEV, POOL, POOL, C), row_weights, col_weights)
        return (totals[0] + term_one, totals[1] + term_two), windows

    stacked = (roi_feat.reshape(block_count, R_DEV, POOL, POOL, C), pre_one.reshape(block_count, R_DEV, POOL, POOL, C), grad_two.reshape(block_count, R_DEV, POOL, POOL, C), roi_rows.reshape(block_count, R_DEV, BOX, POOL), roi_cols.reshape(block_count, R_DEV, BOX, POOL))
    zero_terms = (jnp.zeros((C, 9 * C), jnp.float32), jnp.zeros((C, 9 * C), jnp.float32))
    (term_one, term_two), windows = lax.scan(head_block, zero_terms, stacked)
    windows = windows.reshape(REGIONS, BOX, BOX, C)

    def add_window(region_at, canvas):
        device = region_at // R_DEV
        row_at = (device // N_TX) * TH + off_row[region_at]
        col_at = target_col[region_at, 0] * TW + off_col[region_at]
        corner_at = (row_at.astype(jnp.int32), col_at.astype(jnp.int32), jnp.int32(0))
        current = lax.dynamic_slice(canvas, corner_at, (BOX, BOX, C))
        return lax.dynamic_update_slice(canvas, current + windows[region_at].astype(canvas.dtype), corner_at)

    canvas = lax.fori_loop(0, REGIONS, add_window, jnp.zeros((H + BOX, W + BOX, C), jnp.float32))
    feature_grad = (fpn_grad.astype(jnp.float32) + canvas[:H, :W]).astype(jnp.bfloat16)
    tile_pad = ((1, 1), (1, 1), (0, 0))
    grad_padded = jnp.pad(feature_grad, tile_pad)
    input_padded = jnp.pad(fpn_input, tile_pad)

    def fpn_block(total, block_at):
        row_at = (block_at * TH).astype(jnp.int32)
        grad_rows = lax.dynamic_slice_in_dim(grad_padded, row_at, TH + 2, 0)
        input_rows = lax.dynamic_slice_in_dim(input_padded, row_at, TH + 2, 0)
        back_rows = jnp.dot(window_patches(grad_rows, TH, W, True).reshape(TH * W, 9 * C), flipped_weight(w_fpn), preferred_element_type=jnp.float32).astype(jnp.bfloat16)
        own_grad = lax.dynamic_slice_in_dim(feature_grad, row_at, TH, 0).reshape(TH * W, C)
        total = total + weight_term(own_grad, window_patches(input_rows, TH, W, False).reshape(TH * W, 9 * C))
        return total, back_rows.reshape(TH, W, C)

    term_fpn, blocks_out = lax.scan(fpn_block, jnp.zeros((C, 9 * C), jnp.float32), jnp.arange(N_TY, dtype=jnp.int32))
    grad_fpn_input = blocks_out.reshape(H, W, C)
    return (grad_fpn_input, term_one.reshape(-1), term_two.reshape(-1), term_fpn.reshape(-1))
```

```python
import functools

import jax
import jax.numpy as jnp
from jax import lax
from jax.experimental import pallas as pl
from jax.experimental.pallas import tpu as pltpu
from jax.sharding import PartitionSpec as P

BF = jnp.bfloat16
F32 = jnp.float32
VMEM_BYTES = 56 << 20
NT = (((1,), (1,)), ((), ()))


def ceil_to(value, multiple):
    return -(-value // multiple) * multiple


def slot_rows(pool):
    return ceil_to(pool * pool + 3, 8)


def params():
    return pltpu.CompilerParams(vmem_limit_bytes=VMEM_BYTES)


def cost(flops=1):
    return pl.CostEstimate(flops=int(flops), bytes_accessed=1, transcendentals=0)


def whole(array):
    return pl.BlockSpec(array.shape, lambda *_: (0,) * array.ndim)


def head_body(geometry, target, off_row, off_col, row_ref, col_ref, grad_hbm, pre_hbm, w_two_hbm, w_one_hbm, *rest):
    pool, pitch, regions, capacity, columns, together = geometry
    one_hbm, out = rest[0], rest[1]
    (order, slot_at, held, facts, bare, grads, pres, ones, w_two, w_one, wide, mask, again, packed, taps, sems, out_sems, w_sems) = rest[2:]
    block = (pool + 1) * pitch
    length, rows = together * block + pitch, together * block - pitch

    for j, (src, dst) in enumerate(((w_two_hbm, w_two), (w_one_hbm, w_one))):
        pltpu.make_async_copy(src, dst, w_sems.at[j]).start()
    for q in range(columns):
        held[q] = 0

    def scan(r, count):
        group = target[r]
        rank = held[group]
        held[group] = rank + 1
        order[count] = r
        slot_at[count] = group * capacity + rank
        return count + 1

    count = lax.fori_loop(0, regions, scan, 0)
    steps = (count + together - 1) // together

    def loads(step, which):
        copies = []
        for r in range(together):
            region = order[jnp.minimum(step * together + r, count - 1)]
            for j, (src, dst) in enumerate(((grad_hbm, grads), (pre_hbm, pres))):
                copies.append(pltpu.make_async_copy(src.at[region], dst.at[which, r], sems.at[which, r, j]))
        return copies

    def store(step, which, r):
        region = order[jnp.minimum(step * together + r, count - 1)]
        return pltpu.make_async_copy(
            ones.at[which, pl.ds(r * block, block)],
            one_hbm.at[pl.ds(pl.multiple_of(region * block, block), block)],
            out_sems.at[which, r],
        )

    def settle(step, which):
        for r in range(together):

            @pl.when(step * together + r < count)
            def _(r=r):
                store(step, which, r).wait()

    @pl.when(count > 0)
    def _():
        for copy in loads(0, 0):
            copy.start()

    channels, bins = wide.shape[1], pool * pool
    extent = row_ref.shape[1]
    lane = lax.broadcasted_iota(jnp.int32, (128, channels), 1)
    own = lax.broadcasted_iota(jnp.int32, (128, channels), 0) == lane % pool
    spread = jnp.where(own & (lane < extent * pool), 1.0, 0.0).astype(BF)
    flat = (regions * extent, channels)
    own = lax.broadcasted_iota(jnp.int32, flat, 0) % extent == lax.broadcasted_iota(jnp.int32, flat, 1) // pool
    bare[...] = jnp.zeros_like(bare)
    for j, ref in enumerate((row_ref, col_ref)):
        bare[:, pl.ds(0, pool)] = ref[...].reshape(regions * extent, pool).astype(F32)
        entry = jnp.dot(bare[...].astype(BF), spread, preferred_element_type=F32)
        entry = jnp.where(own, entry, 0.0).reshape(regions, extent, channels)
        facts[j, pl.ds(0, regions), :] = jnp.sum(entry, axis=1)
    lane = lax.broadcasted_iota(jnp.int32, (1, channels), 1)
    out[...] = jnp.zeros_like(out)
    wide[...] = jnp.zeros_like(wide)
    again[...] = jnp.zeros_like(again)
    mask[...] = jnp.zeros_like(mask)
    packed[...] = jnp.zeros_like(packed)
    for which in range(2):
        for r in range(together):
            ones[which, pl.ds((r + 1) * block - pitch, pitch), :] = jnp.zeros((pitch, wide.shape[1]), BF)
    for j, (src, dst) in enumerate(((w_two_hbm, w_two), (w_one_hbm, w_one))):
        pltpu.make_async_copy(src, dst, w_sems.at[j]).wait()

    def conv(source, weight):
        for e in range(3):
            taps[e] = source[pl.ds(7 + e, length), :].astype(BF)
        total = None
        for ey in range(3):
            for ex in range(3):
                term = lax.dot_general(
                    taps[ex, pl.ds(ey * pitch, rows), :],
                    weight[2 - ey, 2 - ex],
                    NT,
                    preferred_element_type=F32,
                )
                total = term if total is None else total + term
        return total

    def turn(step, carry):
        which = step % 2

        @pl.when(step + 1 < steps)
        def _():
            for copy in loads(step + 1, 1 - which):
                copy.start()

        for copy in loads(step, which):
            copy.wait()

        @pl.when(step >= 2)
        def _():
            settle(step - 2, which)

        for r in range(together):
            for y in range(pool):
                at = r * block + y * pitch
                wide[pl.ds(8 + pitch + at, pool), :] = grads[which, r, y].astype(F32)
                mask[pl.ds(at, pool), :] = pres[which, r, y].astype(F32)
        grad_one = jnp.where(mask[pl.ds(0, rows), :] > 0, conv(wide, w_two), 0.0)
        again[pl.ds(8 + pitch, rows), :] = grad_one
        ones[which, pl.ds(0, rows), :] = grad_one.astype(BF)
        for r in range(together):

            @pl.when(step * together + r < count)
            def _(r=r):
                store(step, which, r).start()

        region_grad = conv(again, w_one)
        for r in range(together):
            for y in range(pool):
                at = r * block + y * pitch
                packed[pl.ds(y * pool, pitch), :] = region_grad[at : at + pitch]
            at = jnp.minimum(step * together + r, count - 1)
            region = order[at]
            for j in range(2):
                packed[pl.ds(bins + j, 1), :] = facts[j, pl.ds(region, 1), :]
            place = jnp.where(lane == 0, off_row[region], jnp.where(lane == 1, off_col[region], lane == 2))
            packed[pl.ds(bins + 2, 1), :] = place.astype(F32)
            out[slot_at[at]] = packed[pl.ds(0, out.shape[1]), :].astype(BF)

        return carry

    lax.fori_loop(0, steps, turn, 0)

    @pl.when(steps > 1)
    def _():
        settle(steps - 2, steps % 2)

    @pl.when(steps > 0)
    def _():
        settle(steps - 1, (steps - 1) % 2)


def region_heads(grad_two, pre_one, w_two, w_one, roi_rows, roi_cols, target, off_row, off_col, columns, capacity, together=2):
    regions, pool, _, channels = grad_two.shape
    pitch = ceil_to(pool + 1, 16)
    block = (pool + 1) * pitch
    length = together * block + pitch
    anywhere = pl.BlockSpec(memory_space=pl.ANY)
    smem = pl.BlockSpec(memory_space=pltpu.SMEM)
    vmem = pl.BlockSpec(memory_space=pltpu.VMEM)
    return pl.pallas_call(
        functools.partial(head_body, (pool, pitch, regions, capacity, columns, together)),
        in_specs=[smem] * 3 + [vmem] * 2 + [anywhere] * 4,
        out_specs=[anywhere, vmem],
        out_shape=[
            jax.ShapeDtypeStruct((regions * block, channels), BF),
            jax.ShapeDtypeStruct((columns * capacity, slot_rows(pool), channels), BF),
        ],
        scratch_shapes=[
            pltpu.SMEM((regions,), jnp.int32),
            pltpu.SMEM((regions,), jnp.int32),
            pltpu.SMEM((columns,), jnp.int32),
            pltpu.VMEM((2, ceil_to(regions, 8), channels), F32),
            pltpu.VMEM((regions * roi_rows.shape[1], 128), F32),
            pltpu.VMEM((2, together, pool, pool, channels), BF),
            pltpu.VMEM((2, together, pool, pool, channels), BF),
            pltpu.VMEM((2, together * block, channels), BF),
            pltpu.VMEM(w_two.shape, BF),
            pltpu.VMEM(w_one.shape, BF),
            pltpu.VMEM((length + 16, channels), F32),
            pltpu.VMEM((length, channels), F32),
            pltpu.VMEM((length + 16, channels), F32),
            pltpu.VMEM((pool * pool + pitch, channels), F32),
            pltpu.VMEM((3, length, channels), BF),
            pltpu.SemaphoreType.DMA((2, together, 2)),
            pltpu.SemaphoreType.DMA((2, together)),
            pltpu.SemaphoreType.DMA((2,)),
        ],
        compiler_params=params(),
        cost_estimate=cost(72 * regions * block * channels * channels),
        name="region_heads",
    )(target, off_row, off_col, roi_rows, roi_cols, grad_two, pre_one, w_two, w_one)


def spread_rows(where, source, keep, send, layout):
    chips, highs, share = layout
    core, chip, low, high = where[0] % 2, where[0] // 2, where[1] % 2, where[1] // 2
    for other, out in enumerate((keep, send)):
        for a in range(chips):
            for b in range(2):
                for k in range(highs):
                    block = (((chip ^ a) * 2 + (core ^ other)) * highs + (high ^ k)) * 2 + (low ^ b)
                    place = ((a * 2 + b) * highs + k) * share
                    if share % 8 == 0:
                        rows = source[pl.ds(pl.multiple_of(block * share, 8), share), :]
                    else:
                        rows = source[pl.ds(pl.multiple_of(block * share // 8 * 8, 8), 8), :]
                        rows = pltpu.roll(rows, (8 - block * share % 8) % 8, 0)[:share]
                    out[pl.ds(place, share), :] = rows


def head_weight_body(geometry, where, two_ref, pre_ref, one_hbm, feat_hbm, keep_ref, send_ref, one, feat, turned, wide, taps, product, passed, sems):
    regions, pool, pitch, layout = geometry
    block = (pool + 1) * pitch
    length = turned.shape[1]
    step = pl.program_id(0)
    copies = [pltpu.make_async_copy(one_hbm, one, sems.at[0]), pltpu.make_async_copy(feat_hbm, feat, sems.at[1])]

    def lay_out(ref, relu):
        for r in range(regions):
            for y in range(pool):
                entry = ref[r, y].astype(F32)
                wide[pl.ds(8 + pitch + r * block + y * pitch, pool), :] = jnp.maximum(entry, 0.0) if relu else entry
        for e in range(3):
            taps[e] = wide[pl.ds(7 + e, length + 2 * pitch), :].astype(BF)

    @pl.when(step == 0)
    def _():
        for copy in copies:
            copy.start()
        wide[...] = jnp.zeros_like(wide)
        turned[...] = jnp.zeros_like(turned)
        lay_out(two_ref, False)
        for r in range(regions):
            turned[:, pl.ds(r * block, block)] = taps[1, pl.ds(pitch + r * block, block), :].T
        lay_out(pre_ref, True)

    @pl.when(step == 3)
    def _():
        for copy in copies:
            copy.wait()
        for r in range(regions):
            turned[:, pl.ds(r * block, block)] = one[pl.ds(r * block, block), :].T
        lay_out(feat, False)

    channels = taps.shape[2]
    for ex in range(3):
        patch = taps[ex, pl.ds(pl.multiple_of(step % 3 * pitch, pitch), length), :]
        product[:, ex * channels : (ex + 1) * channels] = jnp.dot(turned[...], patch, preferred_element_type=F32)
    spread_rows(where, product, keep_ref.at[0], passed, layout)
    send_ref[0] = passed[...].astype(BF)


def head_weight_grads(where, layout, grad_two, pre_one, grad_one, roi_feat):
    regions, pool, _, channels = roi_feat.shape
    pitch = ceil_to(pool + 1, 16)
    length = ceil_to(regions * (pool + 1) * pitch, 128)
    anywhere = pl.BlockSpec(memory_space=pl.ANY)
    out = pl.BlockSpec((1, channels // 2, 3 * channels), lambda s: (s // 3, 0, s % 3))
    return pl.pallas_call(
        functools.partial(head_weight_body, (regions, pool, pitch, layout)),
        grid=(6,),
        in_specs=[pl.BlockSpec(memory_space=pltpu.SMEM), whole(grad_two), whole(pre_one), anywhere, anywhere],
        out_specs=[out, out],
        out_shape=[
            jax.ShapeDtypeStruct((2, channels // 2, 9 * channels), F32),
            jax.ShapeDtypeStruct((2, channels // 2, 9 * channels), BF),
        ],
        scratch_shapes=[
            pltpu.VMEM(grad_one.shape, BF),
            pltpu.VMEM(roi_feat.shape, BF),
            pltpu.VMEM((channels, length), BF),
            pltpu.VMEM((length + 2 * pitch + 16, channels), F32),
            pltpu.VMEM((3, length + 2 * pitch, channels), BF),
            pltpu.VMEM((channels, 3 * channels), F32),
            pltpu.VMEM((channels // 2, 3 * channels), F32),
            pltpu.SemaphoreType.DMA((2,)),
        ],
        compiler_params=params(),
        cost_estimate=cost(),
        name="head_weight_grads",
    )(where, grad_two, pre_one, grad_one, roi_feat)


def lay_body(geometry, own_ref, left_ref, right_ref, out_ref, wide):
    rows, pitch, tile_cols = geometry
    wide[...] = jnp.zeros_like(wide)
    for y in range(rows):
        at = 8 + y * pitch
        wide[pl.ds(at, tile_cols), :] = own_ref[y].astype(F32)
        wide[pl.ds(at + tile_cols, pitch - tile_cols), :] = right_ref[y].astype(F32)
    for e in (1, 2):
        out_ref[e] = wide[pl.ds(7 + e, out_ref.shape[1]), :].astype(BF)
    for y in range(rows):
        wide[pl.ds(7 + y * pitch, 1), :] = left_ref[y].astype(F32)
    out_ref[0] = wide[pl.ds(7, out_ref.shape[1]), :].astype(BF)


def lay_out_input(own, left, right):
    rows, tile_cols, channels = own.shape
    pitch = tile_cols + right.shape[1]
    vmem = pl.BlockSpec(memory_space=pltpu.VMEM)
    full = ceil_to(rows, 2)
    return pl.pallas_call(
        functools.partial(lay_body, (rows, pitch, tile_cols)),
        in_specs=[vmem] * 3,
        out_specs=vmem,
        out_shape=jax.ShapeDtypeStruct((3, full * pitch, channels), BF),
        scratch_shapes=[pltpu.VMEM((full * pitch + 16, channels), F32)],
        compiler_params=params(),
        cost_estimate=cost(),
        name="lay_out_input",
    )(own, left, right)


def place_all(geometry, received, start_ref, canvas, row_spread, col_spread, block, numbers, place, sem):
    slots, extent, pool, tile_rows, tile_cols = geometry
    depth, channels = received.shape[1], received.shape[2]
    wide, bins = extent + 8, pool * pool
    facts = received[:, pl.ds(bins // 8 * 8, depth - bins // 8 * 8), :].astype(F32)
    numbers[...] = facts[:, bins % 8 + 2, :128].astype(jnp.int32)
    copy = pltpu.make_async_copy(numbers, place, sem)
    copy.start()
    full = block.shape[0]
    lane = lax.broadcasted_iota(jnp.int32, (channels, full), 1)
    source = lax.broadcasted_iota(jnp.int32, (channels, full), 0) % pool
    own = lax.broadcasted_iota(jnp.int32, (slots, extent, channels), 1) == (
        lax.broadcasted_iota(jnp.int32, (slots, extent, channels), 2) // pool
    )
    for j, (out, part) in enumerate(((row_spread, lane // pool), (col_spread, lane % pool))):
        chosen = jnp.where((part == source) & (lane < bins), 1.0, 0.0).astype(BF)
        entry = jnp.broadcast_to(facts[:, bins % 8 + j : bins % 8 + j + 1, :], (slots, extent, channels))
        entry = jnp.where(own, entry, 0.0).astype(BF).reshape(slots * extent, channels)
        entry = jnp.dot(entry, chosen, preferred_element_type=F32).reshape(slots, extent, full)
        out[:, pl.ds(0, extent), :] = entry
    col_spread[:, pl.ds(extent, 8), :] = jnp.zeros((slots, 8, full), F32)
    block[...] = jnp.zeros_like(block)
    canvas[...] = jnp.zeros_like(canvas)
    canvas[pl.ds(0, tile_rows), pl.ds(0, tile_cols), :] = start_ref[...].astype(F32)
    copy.wait()

    def put(slot, carry):
        @pl.when(place[slot, 2] > 0)
        def _():
            row, col = place[slot, 0], place[slot, 1]
            cols = pltpu.roll(col_spread[slot], col % 8, 0)
            rows = row_spread[slot]
            weights = jnp.concatenate([rows[y : y + 1] * cols for y in range(extent)], axis=0).astype(BF)
            block[pl.ds(0, depth), :] = received[slot]
            window = jnp.dot(weights, block[...], preferred_element_type=F32)
            at = pl.multiple_of(col // 8 * 8, 8)
            for y in range(extent):
                here = (row + y, pl.ds(at, wide))
                canvas[here] = canvas[here] + window[y * wide : (y + 1) * wide]

        return carry

    lax.fori_loop(0, slots, put, 0)


def tile_body(geometry, where, start_ref, received, taps_hbm, canvas, keep_hbm, send_hbm, taps, turned, product, keep, send, row_spread, col_spread, block, numbers, place, sems):
    slots, extent, pool, tile_rows, tile_cols, downs, acrosses, layout = geometry
    rows, pitch, channels = canvas.shape
    load = pltpu.make_async_copy(taps_hbm, taps, sems.at[0])
    load.start()
    place_all(
        (slots, extent, pool, tile_rows, tile_cols), received, start_ref, canvas, row_spread, col_spread, block, numbers, place, sems.at[1]
    )

    @pl.when(where[0] == downs - 1)
    def _():
        canvas[pl.ds(tile_rows, extent)] = jnp.zeros((extent, pitch, channels), F32)

    @pl.when(where[1] == acrosses - 1)
    def _():
        canvas[:, pl.ds(tile_cols, extent), :] = jnp.zeros((rows, extent, channels), F32)

    for y in range(0, rows, 2):
        entry = canvas[pl.ds(y, 2)].reshape(2 * pitch, channels)
        turned[:, pl.ds(y * pitch, 2 * pitch)] = entry.astype(BF).T
    load.wait()
    length = rows * pitch
    for ey in range(3):
        for ex in range(3):
            patch = taps[ex, pl.ds(ey * pitch, length), :]
            product[:, ex * channels : (ex + 1) * channels] = jnp.dot(
                turned[...], patch, preferred_element_type=F32
            )
        at = pl.ds(ey * 3 * channels, 3 * channels)
        spread_rows(where, product, keep.at[:, at], send.at[:, at], layout)
    keep_hbm[0] = keep[...]
    send_hbm[0] = send[...].astype(BF)


def tile_gradient(where, layout, start, received, taps, extent, pool, downs, acrosses):
    tile_rows, tile_cols, channels = start.shape
    slots, depth, _ = received.shape
    rows, pitch = tile_rows + extent, tile_cols + extent
    smem = pl.BlockSpec(memory_space=pltpu.SMEM)
    vmem = pl.BlockSpec(memory_space=pltpu.VMEM)
    geometry = (slots, extent, pool, tile_rows, tile_cols, downs, acrosses, layout)
    return pl.pallas_call(
        functools.partial(tile_body, geometry),
        in_specs=[smem, vmem, vmem, pl.BlockSpec(memory_space=pl.ANY)],
        out_specs=[vmem, vmem, vmem],
        out_shape=[
            jax.ShapeDtypeStruct((rows, pitch, channels), F32),
            jax.ShapeDtypeStruct((1, channels // 2, 9 * channels), F32),
            jax.ShapeDtypeStruct((1, channels // 2, 9 * channels), BF),
        ],
        scratch_shapes=[
            pltpu.VMEM(taps.shape, BF),
            pltpu.VMEM((channels, rows * pitch), BF),
            pltpu.VMEM((channels, 3 * channels), F32),
            pltpu.VMEM((channels // 2, 9 * channels), F32),
            pltpu.VMEM((channels // 2, 9 * channels), F32),
            pltpu.VMEM((slots, extent, ceil_to(depth, 128)), F32),
            pltpu.VMEM((slots, extent + 8, ceil_to(depth, 128)), F32),
            pltpu.VMEM((ceil_to(depth, 128), channels), BF),
            pltpu.VMEM((slots, 128), jnp.int32),
            pltpu.SMEM((slots, 128), jnp.int32),
            pltpu.SemaphoreType.DMA((2,)),
        ],
        compiler_params=params(),
        cost_estimate=cost(36 * rows * pitch * channels * channels),
        name="tile_gradient",
    )(where, start, received, taps)


def tile_input_body(pitch, rows, left_ref, mid_ref, right_ref, weight, out_ref):
    refs = (left_ref, mid_ref, right_ref)
    half = rows // 2
    for part in range(2):
        total = None
        for ey in range(3):
            for ex in range(3):
                term = lax.dot_general(
                    refs[ex][pl.ds((part * half + ey) * pitch, half * pitch), :],
                    weight[2 - ey, 2 - ex],
                    NT,
                    preferred_element_type=F32,
                )
                total = term if total is None else total + term
        out_ref[pl.ds(part * half * pitch, half * pitch), :] = total.astype(BF)


def tile_input_grad(shifted_grads, weight):
    rows, pitch, channels = shifted_grads[0].shape
    rows = rows - 2
    flat = [a.reshape((rows + 2) * pitch, channels) for a in shifted_grads]
    out = pl.pallas_call(
        functools.partial(tile_input_body, pitch, rows),
        out_shape=jax.ShapeDtypeStruct((rows * pitch, channels), BF),
        compiler_params=params(),
        cost_estimate=cost(),
        name="tile_input_grad",
    )(*flat, weight)
    return out.reshape(rows, pitch, channels)


def neighbours(array, axis, by):
    count = lax.axis_size(axis)
    return lax.ppermute(array, axis, [(i, i + by) for i in range(count) if 0 <= i + by < count])


def partner(array, bits_ty, bits_tx):
    down, across = lax.axis_size("ty"), lax.axis_size("tx")
    if bits_ty == 0:
        return lax.ppermute(array, "tx", [(i, i ^ bits_tx) for i in range(across)])
    if bits_tx == 0:
        return lax.ppermute(array, "ty", [(i, i ^ bits_ty) for i in range(down)])
    pairs = [
        (t * across + s, (t ^ bits_ty) * across + (s ^ bits_tx)) for t in range(down) for s in range(across)
    ]
    return lax.ppermute(array, ("ty", "tx"), pairs)


def sum_pairs(keep, send, layout):
    chips, highs, share = layout
    got = partner(send, 1, 0)
    return (keep + got.astype(F32)).reshape(keep.shape[0], chips * 2, highs * share, keep.shape[2])


def sum_chips(total, layout):
    chips, highs, share = layout
    arrived = [
        partner(total[:, 2 * a + b].astype(BF), 2 * a, b) for a in range(chips) for b in range(2) if a or b
    ]
    total = total[:, 0] + sum(got.astype(F32) for got in arrived)
    return total.reshape(total.shape[0], highs, share, total.shape[2])


def sum_rest(total, layout):
    chips, highs, share = layout
    arrived = [partner(total[:, k].astype(BF), 0, 2 * k) for k in range(1, highs)]
    return (total[:, 0] + sum(got.astype(F32) for got in arrived)).reshape(total.shape[0], -1)


def after(value, *earlier):
    return lax.optimization_barrier((value, earlier))[0]


def local(
    roi_feat,
    pre_one,
    grad_two,
    w_one,
    w_two,
    roi_rows,
    roi_cols,
    target_col,
    off_row,
    off_col,
    fpn_input,
    fpn_grad,
    w_fpn,
):
    regions, pool, channels = roi_feat.shape[0], roi_feat.shape[1], roi_feat.shape[3]
    tile_rows, tile_cols = fpn_input.shape[0], fpn_input.shape[1]
    extent = roi_rows.shape[1]
    down, across = lax.axis_size("ty"), lax.axis_size("tx")
    ty, tx = lax.axis_index("ty"), lax.axis_index("tx")
    capacity = max(2, (2 * regions + across - 1) // across)
    layout = (down // 2, across // 2, channels // (down * across))
    where = jnp.stack([ty, tx]).astype(jnp.int32)

    grad_one, sent = region_heads(
        grad_two, pre_one, w_two, w_one, roi_rows, roi_cols, target_col.reshape(-1), off_row, off_col, across, capacity
    )
    received = lax.all_to_all(sent, "tx", 0, 0, tiled=True)

    terms = head_weight_grads(where, layout, grad_two, pre_one, grad_one, roi_feat)
    heads = sum_pairs(*terms, layout)

    above = neighbours(fpn_input[tile_rows - 1 :], "ty", 1)
    below = neighbours(fpn_input[:extent], "ty", -1)
    tall = jnp.concatenate([above, fpn_input, below], axis=0)
    left = neighbours(tall[:, tile_cols - 1 :], "tx", 1)
    right = neighbours(tall[:, :extent], "tx", -1)
    taps = lay_out_input(tall, left, right)

    canvas, *terms = tile_gradient(
        where, layout, after(fpn_grad, heads), received, taps, extent, pool, down, across
    )
    heads = sum_chips(after(heads, canvas), layout)
    total = sum_pairs(*terms, layout)
    canvas = after(canvas, total)
    total = sum_chips(total, layout)
    head_fpn = sum_rest(total, layout)
    heads = sum_rest(after(heads, total), layout)

    spilled = neighbours(canvas[:, tile_cols - 1 : tile_cols + extent - 1].astype(BF), "tx", 1)
    first = neighbours(canvas[:, :1].astype(BF), "tx", -1)
    wide = jnp.pad(canvas[:, : tile_cols + 1], ((0, 0), (1, 0), (0, 0)))
    wide = wide + jnp.pad(spilled.astype(F32), ((0, 0), (0, tile_cols + 2 - extent), (0, 0)))
    wide = wide + jnp.pad(first.astype(F32), ((0, 0), (tile_cols + 1, 0), (0, 0)))
    spilled = neighbours(wide[tile_rows - 1 : tile_rows + extent - 1].astype(BF), "ty", 1)
    first = neighbours(wide[:1].astype(BF), "ty", -1)
    tall = jnp.pad(wide[: tile_rows + 1], ((1, 0), (0, 0), (0, 0)))
    tall = tall + jnp.pad(spilled.astype(F32), ((0, tile_rows + 2 - extent), (0, 0), (0, 0)))
    tall = (tall + jnp.pad(first.astype(F32), ((tile_rows + 1, 0), (0, 0), (0, 0)))).astype(BF)
    input_grad = tile_input_grad([tall[:, e : e + tile_cols] for e in range(3)], w_fpn)
    return (input_grad, heads[1], heads[0], head_fpn[0])


def solution(mesh):
    placed = (
        P(("ty", "tx"), None, None, None),
        P(("ty", "tx"), None, None, None),
        P(("ty", "tx"), None, None, None),
        P(),
        P(),
        P(("ty", "tx"), None, None),
        P(("ty", "tx"), None, None),
        P(("ty", "tx"), None),
        P(("ty", "tx")),
        P(("ty", "tx")),
        P("ty", "tx", None),
        P("ty", "tx", None),
        P(),
    )
    return jax.shard_map(
        local,
        mesh=mesh,
        in_specs=placed,
        out_specs=(P("ty", "tx", None), P(("ty", "tx")), P(("ty", "tx")), P(("ty", "tx"))),
        check_vma=False,
    )
```

```python
import functools

import jax
import jax.numpy as jnp
from jax import lax
from jax.experimental import pallas as pl
from jax.experimental.pallas import tpu as pltpu
from jax.sharding import PartitionSpec as P

BF = jnp.bfloat16
F32 = jnp.float32
VMEM_BYTES = 56 << 20
NT = (((1,), (1,)), ((), ()))


def ceil_to(value, multiple):
    return -(-value // multiple) * multiple


def slot_rows(pool):
    return ceil_to(pool * pool + 3, 8)


def params():
    return pltpu.CompilerParams(vmem_limit_bytes=VMEM_BYTES)


def cost(flops=1):
    return pl.CostEstimate(flops=int(flops), bytes_accessed=1, transcendentals=0)


def whole(array):
    return pl.BlockSpec(array.shape, lambda *_: (0,) * array.ndim)


def head_body(geometry, target, off_row, off_col, row_ref, col_ref, grad_hbm, pre_hbm, w_two_hbm, w_one_hbm, *rest):
    pool, pitch, regions, capacity, columns, together = geometry
    one_hbm, out = rest[0], rest[1]
    (order, slot_at, held, facts, bare, grads, pres, ones, w_two, w_one, wide, mask, again, packed, taps, sems, out_sems, w_sems) = rest[2:]
    block = (pool + 1) * pitch
    length, rows = together * block + pitch, together * block - pitch

    for j, (src, dst) in enumerate(((w_two_hbm, w_two), (w_one_hbm, w_one))):
        pltpu.make_async_copy(src, dst, w_sems.at[j]).start()
    for q in range(columns):
        held[q] = 0

    def scan(r, count):
        group = target[r]
        rank = held[group]
        held[group] = rank + 1
        order[count] = r
        slot_at[count] = group * capacity + rank
        return count + 1

    count = lax.fori_loop(0, regions, scan, 0)
    steps = (count + together - 1) // together

    def loads(step, which):
        copies = []
        for r in range(together):
            region = order[jnp.minimum(step * together + r, count - 1)]
            for j, (src, dst) in enumerate(((grad_hbm, grads), (pre_hbm, pres))):
                copies.append(pltpu.make_async_copy(src.at[region], dst.at[which, r], sems.at[which, r, j]))
        return copies

    def store(step, which, r):
        region = order[jnp.minimum(step * together + r, count - 1)]
        return pltpu.make_async_copy(
            ones.at[which, pl.ds(r * block, block)],
            one_hbm.at[pl.ds(pl.multiple_of(region * block, block), block)],
            out_sems.at[which, r],
        )

    def settle(step, which):
        for r in range(together):

            @pl.when(step * together + r < count)
            def _(r=r):
                store(step, which, r).wait()

    @pl.when(count > 0)
    def _():
        for copy in loads(0, 0):
            copy.start()

    channels, bins = wide.shape[1], pool * pool
    extent = row_ref.shape[1]
    lane = lax.broadcasted_iota(jnp.int32, (128, channels), 1)
    own = lax.broadcasted_iota(jnp.int32, (128, channels), 0) == lane % pool
    spread = jnp.where(own & (lane < extent * pool), 1.0, 0.0).astype(BF)
    flat = (regions * extent, channels)
    own = lax.broadcasted_iota(jnp.int32, flat, 0) % extent == lax.broadcasted_iota(jnp.int32, flat, 1) // pool
    bare[...] = jnp.zeros_like(bare)
    for j, ref in enumerate((row_ref, col_ref)):
        bare[:, pl.ds(0, pool)] = ref[...].reshape(regions * extent, pool).astype(F32)
        entry = jnp.dot(bare[...].astype(BF), spread, preferred_element_type=F32)
        entry = jnp.where(own, entry, 0.0).reshape(regions, extent, channels)
        facts[j, pl.ds(0, regions), :] = jnp.sum(entry, axis=1)
    lane = lax.broadcasted_iota(jnp.int32, (1, channels), 1)
    out[...] = jnp.zeros_like(out)
    wide[...] = jnp.zeros_like(wide)
    again[...] = jnp.zeros_like(again)
    mask[...] = jnp.zeros_like(mask)
    packed[...] = jnp.zeros_like(packed)
    for which in range(2):
        for r in range(together):
            ones[which, pl.ds((r + 1) * block - pitch, pitch), :] = jnp.zeros((pitch, wide.shape[1]), BF)
    for j, (src, dst) in enumerate(((w_two_hbm, w_two), (w_one_hbm, w_one))):
        pltpu.make_async_copy(src, dst, w_sems.at[j]).wait()

    def conv(source, weight):
        for e in range(3):
            taps[e] = source[pl.ds(7 + e, length), :].astype(BF)
        total = None
        for ey in range(3):
            for ex in range(3):
                term = lax.dot_general(
                    taps[ex, pl.ds(ey * pitch, rows), :],
                    weight[2 - ey, 2 - ex],
                    NT,
                    preferred_element_type=F32,
                )
                total = term if total is None else total + term
        return total

    def turn(step, carry):
        which = step % 2

        @pl.when(step + 1 < steps)
        def _():
            for copy in loads(step + 1, 1 - which):
                copy.start()

        for copy in loads(step, which):
            copy.wait()

        @pl.when(step >= 2)
        def _():
            settle(step - 2, which)

        for r in range(together):
            for y in range(pool):
                at = r * block + y * pitch
                wide[pl.ds(8 + pitch + at, pool), :] = grads[which, r, y].astype(F32)
                mask[pl.ds(at, pool), :] = pres[which, r, y].astype(F32)
        grad_one = jnp.where(mask[pl.ds(0, rows), :] > 0, conv(wide, w_two), 0.0)
        again[pl.ds(8 + pitch, rows), :] = grad_one
        ones[which, pl.ds(0, rows), :] = grad_one.astype(BF)
        for r in range(together):

            @pl.when(step * together + r < count)
            def _(r=r):
                store(step, which, r).start()

        region_grad = conv(again, w_one)
        for r in range(together):
            for y in range(pool):
                at = r * block + y * pitch
                packed[pl.ds(y * pool, pitch), :] = region_grad[at : at + pitch]
            at = jnp.minimum(step * together + r, count - 1)
            region = order[at]
            for j in range(2):
                packed[pl.ds(bins + j, 1), :] = facts[j, pl.ds(region, 1), :]
            place = jnp.where(lane == 0, off_row[region], jnp.where(lane == 1, off_col[region], lane == 2))
            packed[pl.ds(bins + 2, 1), :] = place.astype(F32)
            out[slot_at[at]] = packed[pl.ds(0, out.shape[1]), :].astype(BF)

        return carry

    lax.fori_loop(0, steps, turn, 0)

    @pl.when(steps > 1)
    def _():
        settle(steps - 2, steps % 2)

    @pl.when(steps > 0)
    def _():
        settle(steps - 1, (steps - 1) % 2)


def region_heads(grad_two, pre_one, w_two, w_one, roi_rows, roi_cols, target, off_row, off_col, columns, capacity, together=2):
    regions, pool, _, channels = grad_two.shape
    pitch = ceil_to(pool + 1, 16)
    block = (pool + 1) * pitch
    length = together * block + pitch
    anywhere = pl.BlockSpec(memory_space=pl.ANY)
    smem = pl.BlockSpec(memory_space=pltpu.SMEM)
    vmem = pl.BlockSpec(memory_space=pltpu.VMEM)
    return pl.pallas_call(
        functools.partial(head_body, (pool, pitch, regions, capacity, columns, together)),
        in_specs=[smem] * 3 + [vmem] * 2 + [anywhere] * 4,
        out_specs=[anywhere, vmem],
        out_shape=[
            jax.ShapeDtypeStruct((regions * block, channels), BF),
            jax.ShapeDtypeStruct((columns * capacity, slot_rows(pool), channels), BF),
        ],
        scratch_shapes=[
            pltpu.SMEM((regions,), jnp.int32),
            pltpu.SMEM((regions,), jnp.int32),
            pltpu.SMEM((columns,), jnp.int32),
            pltpu.VMEM((2, ceil_to(regions, 8), channels), F32),
            pltpu.VMEM((regions * roi_rows.shape[1], 128), F32),
            pltpu.VMEM((2, together, pool, pool, channels), BF),
            pltpu.VMEM((2, together, pool, pool, channels), BF),
            pltpu.VMEM((2, together * block, channels), BF),
            pltpu.VMEM(w_two.shape, BF),
            pltpu.VMEM(w_one.shape, BF),
            pltpu.VMEM((length + 16, channels), F32),
            pltpu.VMEM((length, channels), F32),
            pltpu.VMEM((length + 16, channels), F32),
            pltpu.VMEM((pool * pool + pitch, channels), F32),
            pltpu.VMEM((3, length, channels), BF),
            pltpu.SemaphoreType.DMA((2, together, 2)),
            pltpu.SemaphoreType.DMA((2, together)),
            pltpu.SemaphoreType.DMA((2,)),
        ],
        compiler_params=params(),
        cost_estimate=cost(72 * regions * block * channels * channels),
        name="region_heads",
    )(target, off_row, off_col, roi_rows, roi_cols, grad_two, pre_one, w_two, w_one)


def spread_rows(where, source, keep, send, layout):
    chips, highs, share = layout
    core, chip, low, high = where[0] % 2, where[0] // 2, where[1] % 2, where[1] // 2
    for other, out in enumerate((keep, send)):
        for a in range(chips):
            for b in range(2):
                for k in range(highs):
                    block = (((chip ^ a) * 2 + (core ^ other)) * highs + (high ^ k)) * 2 + (low ^ b)
                    place = ((a * 2 + b) * highs + k) * share
                    if share % 8 == 0:
                        rows = source[pl.ds(pl.multiple_of(block * share, 8), share), :]
                    else:
                        rows = source[pl.ds(pl.multiple_of(block * share // 8 * 8, 8), 8), :]
                        rows = pltpu.roll(rows, (8 - block * share % 8) % 8, 0)[:share]
                    out[pl.ds(place, share), :] = rows


def head_weight_body(geometry, where, two_ref, pre_ref, one_hbm, feat_hbm, keep_ref, send_ref, one, feat, turned, wide, taps, product, passed, sems):
    regions, pool, pitch, layout = geometry
    block = (pool + 1) * pitch
    length = turned.shape[1]
    step = pl.program_id(0)
    copies = [pltpu.make_async_copy(one_hbm, one, sems.at[0]), pltpu.make_async_copy(feat_hbm, feat, sems.at[1])]

    def lay_out(ref, relu):
        for r in range(regions):
            for y in range(pool):
                entry = ref[r, y].astype(F32)
                wide[pl.ds(8 + pitch + r * block + y * pitch, pool), :] = jnp.maximum(entry, 0.0) if relu else entry
        for e in range(3):
            taps[e] = wide[pl.ds(7 + e, length + 2 * pitch), :].astype(BF)

    @pl.when(step == 0)
    def _():
        for copy in copies:
            copy.start()
        wide[...] = jnp.zeros_like(wide)
        turned[...] = jnp.zeros_like(turned)
        lay_out(two_ref, False)
        for r in range(regions):
            turned[:, pl.ds(r * block, block)] = taps[1, pl.ds(pitch + r * block, block), :].T
        lay_out(pre_ref, True)

    @pl.when(step == 3)
    def _():
        for copy in copies:
            copy.wait()
        for r in range(regions):
            turned[:, pl.ds(r * block, block)] = one[pl.ds(r * block, block), :].T
        lay_out(feat, False)

    channels = taps.shape[2]
    for ex in range(3):
        patch = taps[ex, pl.ds(pl.multiple_of(step % 3 * pitch, pitch), length), :]
        product[:, ex * channels : (ex + 1) * channels] = jnp.dot(turned[...], patch, preferred_element_type=F32)
    spread_rows(where, product, keep_ref.at[0], passed, layout)
    send_ref[0] = passed[...].astype(BF)


def head_weight_grads(where, layout, grad_two, pre_one, grad_one, roi_feat):
    regions, pool, _, channels = roi_feat.shape
    pitch = ceil_to(pool + 1, 16)
    length = ceil_to(regions * (pool + 1) * pitch, 128)
    anywhere = pl.BlockSpec(memory_space=pl.ANY)
    out = pl.BlockSpec((1, channels // 2, 3 * channels), lambda s: (s // 3, 0, s % 3))
    return pl.pallas_call(
        functools.partial(head_weight_body, (regions, pool, pitch, layout)),
        grid=(6,),
        in_specs=[pl.BlockSpec(memory_space=pltpu.SMEM), whole(grad_two), whole(pre_one), anywhere, anywhere],
        out_specs=[out, out],
        out_shape=[
            jax.ShapeDtypeStruct((2, channels // 2, 9 * channels), F32),
            jax.ShapeDtypeStruct((2, channels // 2, 9 * channels), BF),
        ],
        scratch_shapes=[
            pltpu.VMEM(grad_one.shape, BF),
            pltpu.VMEM(roi_feat.shape, BF),
            pltpu.VMEM((channels, length), BF),
            pltpu.VMEM((length + 2 * pitch + 16, channels), F32),
            pltpu.VMEM((3, length + 2 * pitch, channels), BF),
            pltpu.VMEM((channels, 3 * channels), F32),
            pltpu.VMEM((channels // 2, 3 * channels), F32),
            pltpu.SemaphoreType.DMA((2,)),
        ],
        compiler_params=params(),
        cost_estimate=cost(),
        name="head_weight_grads",
    )(where, grad_two, pre_one, grad_one, roi_feat)


def lay_body(geometry, own_ref, left_ref, right_ref, out_ref, wide):
    rows, pitch, tile_cols = geometry
    wide[...] = jnp.zeros_like(wide)
    for y in range(rows):
        at = 8 + y * pitch
        wide[pl.ds(at, tile_cols), :] = own_ref[y].astype(F32)
        wide[pl.ds(at + tile_cols, pitch - tile_cols), :] = right_ref[y].astype(F32)
    for e in (1, 2):
        out_ref[e] = wide[pl.ds(7 + e, out_ref.shape[1]), :].astype(BF)
    for y in range(rows):
        wide[pl.ds(7 + y * pitch, 1), :] = left_ref[y].astype(F32)
    out_ref[0] = wide[pl.ds(7, out_ref.shape[1]), :].astype(BF)


def lay_out_input(own, left, right):
    rows, tile_cols, channels = own.shape
    pitch = tile_cols + right.shape[1]
    vmem = pl.BlockSpec(memory_space=pltpu.VMEM)
    full = ceil_to(rows, 2)
    return pl.pallas_call(
        functools.partial(lay_body, (rows, pitch, tile_cols)),
        in_specs=[vmem] * 3,
        out_specs=vmem,
        out_shape=jax.ShapeDtypeStruct((3, full * pitch, channels), BF),
        scratch_shapes=[pltpu.VMEM((full * pitch + 16, channels), F32)],
        compiler_params=params(),
        cost_estimate=cost(),
        name="lay_out_input",
    )(own, left, right)


def place_all(geometry, received, start_ref, canvas, row_spread, col_spread, block, numbers, place, sem):
    slots, extent, pool, tile_rows, tile_cols = geometry
    depth, channels = received.shape[1], received.shape[2]
    wide, bins = extent + 8, pool * pool
    facts = received[:, pl.ds(bins // 8 * 8, depth - bins // 8 * 8), :].astype(F32)
    numbers[...] = facts[:, bins % 8 + 2, :128].astype(jnp.int32)
    copy = pltpu.make_async_copy(numbers, place, sem)
    copy.start()
    full = block.shape[0]
    lane = lax.broadcasted_iota(jnp.int32, (channels, full), 1)
    source = lax.broadcasted_iota(jnp.int32, (channels, full), 0) % pool
    own = lax.broadcasted_iota(jnp.int32, (slots, extent, channels), 1) == (
        lax.broadcasted_iota(jnp.int32, (slots, extent, channels), 2) // pool
    )
    for j, (out, part) in enumerate(((row_spread, lane // pool), (col_spread, lane % pool))):
        chosen = jnp.where((part == source) & (lane < bins), 1.0, 0.0).astype(BF)
        entry = jnp.broadcast_to(facts[:, bins % 8 + j : bins % 8 + j + 1, :], (slots, extent, channels))
        entry = jnp.where(own, entry, 0.0).astype(BF).reshape(slots * extent, channels)
        entry = jnp.dot(entry, chosen, preferred_element_type=F32).reshape(slots, extent, full)
        out[:, pl.ds(0, extent), :] = entry
    col_spread[:, pl.ds(extent, 8), :] = jnp.zeros((slots, 8, full), F32)
    block[...] = jnp.zeros_like(block)
    canvas[...] = jnp.zeros_like(canvas)
    canvas[pl.ds(0, tile_rows), pl.ds(0, tile_cols), :] = start_ref[...].astype(F32)
    copy.wait()

    def put(slot, carry):
        @pl.when(place[slot, 2] > 0)
        def _():
            row, col = place[slot, 0], place[slot, 1]
            cols = pltpu.roll(col_spread[slot], col % 8, 0)
            rows = row_spread[slot]
            weights = jnp.concatenate([rows[y : y + 1] * cols for y in range(extent)], axis=0).astype(BF)
            block[pl.ds(0, depth), :] = received[slot]
            window = jnp.dot(weights, block[...], preferred_element_type=F32)
            at = pl.multiple_of(col // 8 * 8, 8)
            for y in range(extent):
                here = (row + y, pl.ds(at, wide))
                canvas[here] = canvas[here] + window[y * wide : (y + 1) * wide]

        return carry

    lax.fori_loop(0, slots, put, 0)


def tile_body(geometry, where, start_ref, received, taps_hbm, canvas, keep_hbm, send_hbm, taps, turned, product, keep, send, row_spread, col_spread, block, numbers, place, sems):
    slots, extent, pool, tile_rows, tile_cols, downs, acrosses, layout = geometry
    rows, pitch, channels = canvas.shape
    load = pltpu.make_async_copy(taps_hbm, taps, sems.at[0])
    load.start()
    place_all(
        (slots, extent, pool, tile_rows, tile_cols), received, start_ref, canvas, row_spread, col_spread, block, numbers, place, sems.at[1]
    )

    @pl.when(where[0] == downs - 1)
    def _():
        canvas[pl.ds(tile_rows, extent)] = jnp.zeros((extent, pitch, channels), F32)

    @pl.when(where[1] == acrosses - 1)
    def _():
        canvas[:, pl.ds(tile_cols, extent), :] = jnp.zeros((rows, extent, channels), F32)

    for y in range(0, rows, 2):
        entry = canvas[pl.ds(y, 2)].reshape(2 * pitch, channels)
        turned[:, pl.ds(y * pitch, 2 * pitch)] = entry.astype(BF).T
    load.wait()
    length = rows * pitch
    for ey in range(3):
        for ex in range(3):
            patch = taps[ex, pl.ds(ey * pitch, length), :]
            product[:, ex * channels : (ex + 1) * channels] = jnp.dot(
                turned[...], patch, preferred_element_type=F32
            )
        at = pl.ds(ey * 3 * channels, 3 * channels)
        spread_rows(where, product, keep.at[:, at], send.at[:, at], layout)
    keep_hbm[0] = keep[...]
    send_hbm[0] = send[...].astype(BF)


def tile_gradient(where, layout, start, received, taps, extent, pool, downs, acrosses):
    tile_rows, tile_cols, channels = start.shape
    slots, depth, _ = received.shape
    rows, pitch = tile_rows + extent, tile_cols + extent
    smem = pl.BlockSpec(memory_space=pltpu.SMEM)
    vmem = pl.BlockSpec(memory_space=pltpu.VMEM)
    geometry = (slots, extent, pool, tile_rows, tile_cols, downs, acrosses, layout)
    return pl.pallas_call(
        functools.partial(tile_body, geometry),
        in_specs=[smem, vmem, vmem, pl.BlockSpec(memory_space=pl.ANY)],
        out_specs=[vmem, vmem, vmem],
        out_shape=[
            jax.ShapeDtypeStruct((rows, pitch, channels), F32),
            jax.ShapeDtypeStruct((1, channels // 2, 9 * channels), F32),
            jax.ShapeDtypeStruct((1, channels // 2, 9 * channels), BF),
        ],
        scratch_shapes=[
            pltpu.VMEM(taps.shape, BF),
            pltpu.VMEM((channels, rows * pitch), BF),
            pltpu.VMEM((channels, 3 * channels), F32),
            pltpu.VMEM((channels // 2, 9 * channels), F32),
            pltpu.VMEM((channels // 2, 9 * channels), F32),
            pltpu.VMEM((slots, extent, ceil_to(depth, 128)), F32),
            pltpu.VMEM((slots, extent + 8, ceil_to(depth, 128)), F32),
            pltpu.VMEM((ceil_to(depth, 128), channels), BF),
            pltpu.VMEM((slots, 128), jnp.int32),
            pltpu.SMEM((slots, 128), jnp.int32),
            pltpu.SemaphoreType.DMA((2,)),
        ],
        compiler_params=params(),
        cost_estimate=cost(36 * rows * pitch * channels * channels),
        name="tile_gradient",
    )(where, start, received, taps)


def tile_input_body(pitch, rows, left_ref, mid_ref, right_ref, weight, out_ref):
    refs = (left_ref, mid_ref, right_ref)
    half = rows // 2
    for part in range(2):
        total = None
        for ey in range(3):
            for ex in range(3):
                term = lax.dot_general(
                    refs[ex][pl.ds((part * half + ey) * pitch, half * pitch), :],
                    weight[2 - ey, 2 - ex],
                    NT,
                    preferred_element_type=F32,
                )
                total = term if total is None else total + term
        out_ref[pl.ds(part * half * pitch, half * pitch), :] = total.astype(BF)


def tile_input_grad(shifted_grads, weight):
    rows, pitch, channels = shifted_grads[0].shape
    rows = rows - 2
    flat = [a.reshape((rows + 2) * pitch, channels) for a in shifted_grads]
    out = pl.pallas_call(
        functools.partial(tile_input_body, pitch, rows),
        out_shape=jax.ShapeDtypeStruct((rows * pitch, channels), BF),
        compiler_params=params(),
        cost_estimate=cost(),
        name="tile_input_grad",
    )(*flat, weight)
    return out.reshape(rows, pitch, channels)


def neighbours(array, axis, by):
    count = lax.axis_size(axis)
    return lax.ppermute(array, axis, [(i, i + by) for i in range(count) if 0 <= i + by < count])


def partner(array, bits_ty, bits_tx):
    down, across = lax.axis_size("ty"), lax.axis_size("tx")
    if bits_ty == 0:
        return lax.ppermute(array, "tx", [(i, i ^ bits_tx) for i in range(across)])
    if bits_tx == 0:
        return lax.ppermute(array, "ty", [(i, i ^ bits_ty) for i in range(down)])
    pairs = [
        (t * across + s, (t ^ bits_ty) * across + (s ^ bits_tx)) for t in range(down) for s in range(across)
    ]
    return lax.ppermute(array, ("ty", "tx"), pairs)


def sum_pairs(keep, send, layout):
    chips, highs, share = layout
    got = partner(send, 1, 0)
    return (keep + got.astype(F32)).reshape(keep.shape[0], chips * 2, highs * share, keep.shape[2])


def sum_chips(total, layout):
    chips, highs, share = layout
    arrived = [
        partner(total[:, 2 * a + b].astype(BF), 2 * a, b) for a in range(chips) for b in range(2) if a or b
    ]
    total = total[:, 0] + sum(got.astype(F32) for got in arrived)
    return total.reshape(total.shape[0], highs, share, total.shape[2])


def sum_rest(total, layout):
    chips, highs, share = layout
    arrived = [partner(total[:, k].astype(BF), 0, 2 * k) for k in range(1, highs)]
    return (total[:, 0] + sum(got.astype(F32) for got in arrived)).reshape(total.shape[0], -1)


def after(value, *earlier):
    return lax.optimization_barrier((value, earlier))[0]


def local(
    roi_feat,
    pre_one,
    grad_two,
    w_one,
    w_two,
    roi_rows,
    roi_cols,
    target_col,
    off_row,
    off_col,
    fpn_input,
    fpn_grad,
    w_fpn,
):
    regions, pool, channels = roi_feat.shape[0], roi_feat.shape[1], roi_feat.shape[3]
    tile_rows, tile_cols = fpn_input.shape[0], fpn_input.shape[1]
    extent = roi_rows.shape[1]
    down, across = lax.axis_size("ty"), lax.axis_size("tx")
    ty, tx = lax.axis_index("ty"), lax.axis_index("tx")
    capacity = max(2, (2 * regions + across - 1) // across)
    layout = (down // 2, across // 2, channels // (down * across))
    where = jnp.stack([ty, tx]).astype(jnp.int32)

    grad_one, sent = region_heads(
        grad_two, pre_one, w_two, w_one, roi_rows, roi_cols, target_col.reshape(-1), off_row, off_col, across, capacity
    )
    received = lax.all_to_all(sent, "tx", 0, 0, tiled=True)

    terms = head_weight_grads(where, layout, grad_two, pre_one, grad_one, roi_feat)
    heads = sum_pairs(*terms, layout)

    above = neighbours(fpn_input[tile_rows - 1 :], "ty", 1)
    below = neighbours(fpn_input[:extent], "ty", -1)
    tall = jnp.concatenate([above, fpn_input, below], axis=0)
    left = neighbours(tall[:, tile_cols - 1 :], "tx", 1)
    right = neighbours(tall[:, :extent], "tx", -1)
    taps = lay_out_input(tall, left, right)

    heads = sum_chips(heads, layout)
    canvas, *terms = tile_gradient(
        where, layout, after(fpn_grad, heads), received, taps, extent, pool, down, across
    )
    total = sum_pairs(*terms, layout)
    canvas = after(canvas, total)
    total = sum_chips(total, layout)

    spilled = neighbours(canvas[:, tile_cols - 1 : tile_cols + extent - 1].astype(BF), "tx", 1)
    first = neighbours(canvas[:, :1].astype(BF), "tx", -1)
    wide = jnp.pad(canvas[:, : tile_cols + 1], ((0, 0), (1, 0), (0, 0)))
    wide = wide + jnp.pad(spilled.astype(F32), ((0, 0), (0, tile_cols + 2 - extent), (0, 0)))
    wide = wide + jnp.pad(first.astype(F32), ((0, 0), (tile_cols + 1, 0), (0, 0)))
    head_fpn = sum_rest(after(total, wide), layout)
    heads = sum_rest(after(heads, wide), layout)
    spilled = neighbours(wide[tile_rows - 1 : tile_rows + extent - 1].astype(BF), "ty", 1)
    first = neighbours(wide[:1].astype(BF), "ty", -1)
    tall = jnp.pad(wide[: tile_rows + 1], ((1, 0), (0, 0), (0, 0)))
    tall = tall + jnp.pad(spilled.astype(F32), ((0, tile_rows + 2 - extent), (0, 0), (0, 0)))
    tall = (tall + jnp.pad(first.astype(F32), ((tile_rows + 1, 0), (0, 0), (0, 0)))).astype(BF)
    input_grad = tile_input_grad([tall[:, e : e + tile_cols] for e in range(3)], w_fpn)
    return (input_grad, heads[1], heads[0], head_fpn[0])


def solution(mesh):
    placed = (
        P(("ty", "tx"), None, None, None),
        P(("ty", "tx"), None, None, None),
        P(("ty", "tx"), None, None, None),
        P(),
        P(),
        P(("ty", "tx"), None, None),
        P(("ty", "tx"), None, None),
        P(("ty", "tx"), None),
        P(("ty", "tx")),
        P(("ty", "tx")),
        P("ty", "tx", None),
        P("ty", "tx", None),
        P(),
    )
    return jax.shard_map(
        local,
        mesh=mesh,
        in_specs=placed,
        out_specs=(P("ty", "tx", None), P(("ty", "tx")), P(("ty", "tx")), P(("ty", "tx"))),
        check_vma=False,
    )
```

```python
import functools

import jax
import jax.numpy as jnp
from jax import lax
from jax.experimental import pallas as pl
from jax.experimental.pallas import tpu as pltpu
from jax.sharding import PartitionSpec as P

BF = jnp.bfloat16
F32 = jnp.float32
VMEM_BYTES = 56 << 20
NT = (((1,), (1,)), ((), ()))


def ceil_to(value, multiple):
    return -(-value // multiple) * multiple


def slot_rows(pool):
    return ceil_to(pool * pool + 3, 8)


def params():
    return pltpu.CompilerParams(vmem_limit_bytes=VMEM_BYTES)


def cost(flops=1):
    return pl.CostEstimate(flops=int(flops), bytes_accessed=1, transcendentals=0)


def whole(array):
    return pl.BlockSpec(array.shape, lambda *_: (0,) * array.ndim)


def head_body(geometry, target, off_row, off_col, row_ref, col_ref, grad_hbm, pre_hbm, w_two_hbm, w_one_hbm, *rest):
    pool, pitch, regions, capacity, columns, together = geometry
    one_hbm, out = rest[0], rest[1]
    (order, slot_at, held, facts, bare, grads, pres, ones, w_two, w_one, wide, mask, again, packed, taps, sems, out_sems, w_sems) = rest[2:]
    block = (pool + 1) * pitch
    length, rows = together * block + pitch, together * block - pitch

    for j, (src, dst) in enumerate(((w_two_hbm, w_two), (w_one_hbm, w_one))):
        pltpu.make_async_copy(src, dst, w_sems.at[j]).start()
    for q in range(columns):
        held[q] = 0

    def scan(r, count):
        group = target[r]
        rank = held[group]
        held[group] = rank + 1
        order[count] = r
        slot_at[count] = group * capacity + rank
        return count + 1

    count = lax.fori_loop(0, regions, scan, 0)
    steps = (count + together - 1) // together

    def loads(step, which):
        copies = []
        for r in range(together):
            region = order[jnp.minimum(step * together + r, count - 1)]
            for j, (src, dst) in enumerate(((grad_hbm, grads), (pre_hbm, pres))):
                copies.append(pltpu.make_async_copy(src.at[region], dst.at[which, r], sems.at[which, r, j]))
        return copies

    def store(step, which, r):
        region = order[jnp.minimum(step * together + r, count - 1)]
        return pltpu.make_async_copy(
            ones.at[which, pl.ds(r * block, block)],
            one_hbm.at[pl.ds(pl.multiple_of(region * block, block), block)],
            out_sems.at[which, r],
        )

    def settle(step, which):
        for r in range(together):

            @pl.when(step * together + r < count)
            def _(r=r):
                store(step, which, r).wait()

    @pl.when(count > 0)
    def _():
        for copy in loads(0, 0):
            copy.start()

    channels, bins = wide.shape[1], pool * pool
    extent = row_ref.shape[1]
    lane = lax.broadcasted_iota(jnp.int32, (128, channels), 1)
    own = lax.broadcasted_iota(jnp.int32, (128, channels), 0) == lane % pool
    spread = jnp.where(own & (lane < extent * pool), 1.0, 0.0).astype(BF)
    flat = (regions * extent, channels)
    own = lax.broadcasted_iota(jnp.int32, flat, 0) % extent == lax.broadcasted_iota(jnp.int32, flat, 1) // pool
    bare[...] = jnp.zeros_like(bare)
    for j, ref in enumerate((row_ref, col_ref)):
        bare[:, pl.ds(0, pool)] = ref[...].reshape(regions * extent, pool).astype(F32)
        entry = jnp.dot(bare[...].astype(BF), spread, preferred_element_type=F32)
        entry = jnp.where(own, entry, 0.0).reshape(regions, extent, channels)
        facts[j, pl.ds(0, regions), :] = jnp.sum(entry, axis=1)
    lane = lax.broadcasted_iota(jnp.int32, (1, channels), 1)
    out[...] = jnp.zeros_like(out)
    wide[...] = jnp.zeros_like(wide)
    again[...] = jnp.zeros_like(again)
    mask[...] = jnp.zeros_like(mask)
    packed[...] = jnp.zeros_like(packed)
    for which in range(2):
        for r in range(together):
            ones[which, pl.ds((r + 1) * block - pitch, pitch), :] = jnp.zeros((pitch, wide.shape[1]), BF)
    for j, (src, dst) in enumerate(((w_two_hbm, w_two), (w_one_hbm, w_one))):
        pltpu.make_async_copy(src, dst, w_sems.at[j]).wait()

    def conv(source, weight):
        for e in range(3):
            taps[e] = source[pl.ds(7 + e, length), :].astype(BF)
        total = None
        for ey in range(3):
            for ex in range(3):
                term = lax.dot_general(
                    taps[ex, pl.ds(ey * pitch, rows), :],
                    weight[2 - ey, 2 - ex],
                    NT,
                    preferred_element_type=F32,
                )
                total = term if total is None else total + term
        return total

    def turn(step, carry):
        which = step % 2

        @pl.when(step + 1 < steps)
        def _():
            for copy in loads(step + 1, 1 - which):
                copy.start()

        for copy in loads(step, which):
            copy.wait()

        @pl.when(step >= 2)
        def _():
            settle(step - 2, which)

        for r in range(together):
            for y in range(pool):
                at = r * block + y * pitch
                wide[pl.ds(8 + pitch + at, pool), :] = grads[which, r, y].astype(F32)
                mask[pl.ds(at, pool), :] = pres[which, r, y].astype(F32)
        grad_one = jnp.where(mask[pl.ds(0, rows), :] > 0, conv(wide, w_two), 0.0)
        again[pl.ds(8 + pitch, rows), :] = grad_one
        ones[which, pl.ds(0, rows), :] = grad_one.astype(BF)
        for r in range(together):

            @pl.when(step * together + r < count)
            def _(r=r):
                store(step, which, r).start()

        region_grad = conv(again, w_one)
        for r in range(together):
            for y in range(pool):
                at = r * block + y * pitch
                packed[pl.ds(y * pool, pitch), :] = region_grad[at : at + pitch]
            at = jnp.minimum(step * together + r, count - 1)
            region = order[at]
            for j in range(2):
                packed[pl.ds(bins + j, 1), :] = facts[j, pl.ds(region, 1), :]
            place = jnp.where(lane == 0, off_row[region], jnp.where(lane == 1, off_col[region], lane == 2))
            packed[pl.ds(bins + 2, 1), :] = place.astype(F32)
            out[slot_at[at]] = packed[pl.ds(0, out.shape[1]), :].astype(BF)

        return carry

    lax.fori_loop(0, steps, turn, 0)

    @pl.when(steps > 1)
    def _():
        settle(steps - 2, steps % 2)

    @pl.when(steps > 0)
    def _():
        settle(steps - 1, (steps - 1) % 2)


def region_heads(grad_two, pre_one, w_two, w_one, roi_rows, roi_cols, target, off_row, off_col, columns, capacity, together=2):
    regions, pool, _, channels = grad_two.shape
    pitch = ceil_to(pool + 1, 16)
    block = (pool + 1) * pitch
    length = together * block + pitch
    anywhere = pl.BlockSpec(memory_space=pl.ANY)
    smem = pl.BlockSpec(memory_space=pltpu.SMEM)
    vmem = pl.BlockSpec(memory_space=pltpu.VMEM)
    return pl.pallas_call(
        functools.partial(head_body, (pool, pitch, regions, capacity, columns, together)),
        in_specs=[smem] * 3 + [vmem] * 2 + [anywhere] * 4,
        out_specs=[anywhere, vmem],
        out_shape=[
            jax.ShapeDtypeStruct((regions * block, channels), BF),
            jax.ShapeDtypeStruct((columns * capacity, slot_rows(pool), channels), BF),
        ],
        scratch_shapes=[
            pltpu.SMEM((regions,), jnp.int32),
            pltpu.SMEM((regions,), jnp.int32),
            pltpu.SMEM((columns,), jnp.int32),
            pltpu.VMEM((2, ceil_to(regions, 8), channels), F32),
            pltpu.VMEM((regions * roi_rows.shape[1], 128), F32),
            pltpu.VMEM((2, together, pool, pool, channels), BF),
            pltpu.VMEM((2, together, pool, pool, channels), BF),
            pltpu.VMEM((2, together * block, channels), BF),
            pltpu.VMEM(w_two.shape, BF),
            pltpu.VMEM(w_one.shape, BF),
            pltpu.VMEM((length + 16, channels), F32),
            pltpu.VMEM((length, channels), F32),
            pltpu.VMEM((length + 16, channels), F32),
            pltpu.VMEM((pool * pool + pitch, channels), F32),
            pltpu.VMEM((3, length, channels), BF),
            pltpu.SemaphoreType.DMA((2, together, 2)),
            pltpu.SemaphoreType.DMA((2, together)),
            pltpu.SemaphoreType.DMA((2,)),
        ],
        compiler_params=params(),
        cost_estimate=cost(72 * regions * block * channels * channels),
        name="region_heads",
    )(target, off_row, off_col, roi_rows, roi_cols, grad_two, pre_one, w_two, w_one)


def spread_rows(where, source, keep, send, layout):
    chips, highs, share = layout
    core, chip, low, high = where[0] % 2, where[0] // 2, where[1] % 2, where[1] // 2
    for other, out in enumerate((keep, send)):
        for a in range(chips):
            for b in range(2):
                for k in range(highs):
                    block = (((chip ^ a) * 2 + (core ^ other)) * highs + (high ^ k)) * 2 + (low ^ b)
                    place = ((a * 2 + b) * highs + k) * share
                    if share % 8 == 0:
                        rows = source[pl.ds(pl.multiple_of(block * share, 8), share), :]
                    else:
                        rows = source[pl.ds(pl.multiple_of(block * share // 8 * 8, 8), 8), :]
                        rows = pltpu.roll(rows, (8 - block * share % 8) % 8, 0)[:share]
                    out[pl.ds(place, share), :] = rows


def head_weight_body(geometry, where, two_ref, pre_ref, one_hbm, feat_hbm, keep_ref, send_ref, one, feat, turned, wide, taps, product, passed, sems):
    regions, pool, pitch, layout = geometry
    block = (pool + 1) * pitch
    length = turned.shape[1]
    step = pl.program_id(0)
    copies = [pltpu.make_async_copy(one_hbm, one, sems.at[0]), pltpu.make_async_copy(feat_hbm, feat, sems.at[1])]

    def lay_out(ref, relu):
        for r in range(regions):
            for y in range(pool):
                entry = ref[r, y].astype(F32)
                wide[pl.ds(8 + pitch + r * block + y * pitch, pool), :] = jnp.maximum(entry, 0.0) if relu else entry
        for e in range(3):
            taps[e] = wide[pl.ds(7 + e, length + 2 * pitch), :].astype(BF)

    @pl.when(step == 0)
    def _():
        for copy in copies:
            copy.start()
        wide[...] = jnp.zeros_like(wide)
        turned[...] = jnp.zeros_like(turned)
        lay_out(two_ref, False)
        for r in range(regions):
            turned[:, pl.ds(r * block, block)] = taps[1, pl.ds(pitch + r * block, block), :].T
        lay_out(pre_ref, True)

    @pl.when(step == 3)
    def _():
        for copy in copies:
            copy.wait()
        for r in range(regions):
            turned[:, pl.ds(r * block, block)] = one[pl.ds(r * block, block), :].T
        lay_out(feat, False)

    channels = taps.shape[2]
    for ex in range(3):
        patch = taps[ex, pl.ds(pl.multiple_of(step % 3 * pitch, pitch), length), :]
        product[:, ex * channels : (ex + 1) * channels] = jnp.dot(turned[...], patch, preferred_element_type=F32)
    spread_rows(where, product, keep_ref.at[0], passed, layout)
    send_ref[0] = passed[...].astype(BF)


def head_weight_grads(where, layout, grad_two, pre_one, grad_one, roi_feat):
    regions, pool, _, channels = roi_feat.shape
    pitch = ceil_to(pool + 1, 16)
    length = ceil_to(regions * (pool + 1) * pitch, 128)
    anywhere = pl.BlockSpec(memory_space=pl.ANY)
    out = pl.BlockSpec((1, channels // 2, 3 * channels), lambda s: (s // 3, 0, s % 3))
    return pl.pallas_call(
        functools.partial(head_weight_body, (regions, pool, pitch, layout)),
        grid=(6,),
        in_specs=[pl.BlockSpec(memory_space=pltpu.SMEM), whole(grad_two), whole(pre_one), anywhere, anywhere],
        out_specs=[out, out],
        out_shape=[
            jax.ShapeDtypeStruct((2, channels // 2, 9 * channels), F32),
            jax.ShapeDtypeStruct((2, channels // 2, 9 * channels), BF),
        ],
        scratch_shapes=[
            pltpu.VMEM(grad_one.shape, BF),
            pltpu.VMEM(roi_feat.shape, BF),
            pltpu.VMEM((channels, length), BF),
            pltpu.VMEM((length + 2 * pitch + 16, channels), F32),
            pltpu.VMEM((3, length + 2 * pitch, channels), BF),
            pltpu.VMEM((channels, 3 * channels), F32),
            pltpu.VMEM((channels // 2, 3 * channels), F32),
            pltpu.SemaphoreType.DMA((2,)),
        ],
        compiler_params=params(),
        cost_estimate=cost(),
        name="head_weight_grads",
    )(where, grad_two, pre_one, grad_one, roi_feat)


def lay_out(geometry, own_ref, left_ref, right_ref, out_ref, wide):
    rows, pitch, tile_cols = geometry
    wide[...] = jnp.zeros_like(wide)
    for y in range(rows):
        at = 8 + y * pitch
        wide[pl.ds(at, tile_cols), :] = own_ref[y].astype(F32)
        wide[pl.ds(at + tile_cols, pitch - tile_cols), :] = right_ref[y].astype(F32)
    for e in (1, 2):
        out_ref[e] = wide[pl.ds(7 + e, out_ref.shape[1]), :].astype(BF)
    for y in range(rows):
        wide[pl.ds(7 + y * pitch, 1), :] = left_ref[y].astype(F32)
    out_ref[0] = wide[pl.ds(7, out_ref.shape[1]), :].astype(BF)


def place_all(geometry, received, start_ref, canvas, row_spread, col_spread, block, numbers, place, sem):
    slots, extent, pool, tile_rows, tile_cols = geometry
    depth, channels = received.shape[1], received.shape[2]
    wide, bins = extent + 8, pool * pool
    facts = received[:, pl.ds(bins // 8 * 8, depth - bins // 8 * 8), :].astype(F32)
    numbers[...] = facts[:, bins % 8 + 2, :128].astype(jnp.int32)
    copy = pltpu.make_async_copy(numbers, place, sem)
    copy.start()
    full = block.shape[0]
    lane = lax.broadcasted_iota(jnp.int32, (channels, full), 1)
    source = lax.broadcasted_iota(jnp.int32, (channels, full), 0) % pool
    own = lax.broadcasted_iota(jnp.int32, (slots, extent, channels), 1) == (
        lax.broadcasted_iota(jnp.int32, (slots, extent, channels), 2) // pool
    )
    for j, (out, part) in enumerate(((row_spread, lane // pool), (col_spread, lane % pool))):
        chosen = jnp.where((part == source) & (lane < bins), 1.0, 0.0).astype(BF)
        entry = jnp.broadcast_to(facts[:, bins % 8 + j : bins % 8 + j + 1, :], (slots, extent, channels))
        entry = jnp.where(own, entry, 0.0).astype(BF).reshape(slots * extent, channels)
        entry = jnp.dot(entry, chosen, preferred_element_type=F32).reshape(slots, extent, full)
        out[:, pl.ds(0, extent), :] = entry
    col_spread[:, pl.ds(extent, 8), :] = jnp.zeros((slots, 8, full), F32)
    block[...] = jnp.zeros_like(block)
    canvas[...] = jnp.zeros_like(canvas)
    canvas[pl.ds(0, tile_rows), pl.ds(0, tile_cols), :] = start_ref[...].astype(F32)
    copy.wait()

    def put(slot, carry):
        @pl.when(place[slot, 2] > 0)
        def _():
            row, col = place[slot, 0], place[slot, 1]
            cols = pltpu.roll(col_spread[slot], col % 8, 0)
            rows = row_spread[slot]
            weights = jnp.concatenate([rows[y : y + 1] * cols for y in range(extent)], axis=0).astype(BF)
            block[pl.ds(0, depth), :] = received[slot]
            window = jnp.dot(weights, block[...], preferred_element_type=F32)
            at = pl.multiple_of(col // 8 * 8, 8)
            for y in range(extent):
                here = (row + y, pl.ds(at, wide))
                canvas[here] = canvas[here] + window[y * wide : (y + 1) * wide]

        return carry

    lax.fori_loop(0, slots, put, 0)


def tile_body(geometry, where, start_ref, received, own_ref, left_ref, right_ref, canvas, keep_hbm, send_hbm, taps, wide, turned, product, keep, send, row_spread, col_spread, block, numbers, place, sems):
    slots, extent, pool, tile_rows, tile_cols, downs, acrosses, layout = geometry
    rows, pitch, channels = canvas.shape
    place_all(
        (slots, extent, pool, tile_rows, tile_cols), received, start_ref, canvas, row_spread, col_spread, block, numbers, place, sems.at[0]
    )

    @pl.when(where[0] == downs - 1)
    def _():
        canvas[pl.ds(tile_rows, extent)] = jnp.zeros((extent, pitch, channels), F32)

    @pl.when(where[1] == acrosses - 1)
    def _():
        canvas[:, pl.ds(tile_cols, extent), :] = jnp.zeros((rows, extent, channels), F32)

    for y in range(0, rows, 2):
        entry = canvas[pl.ds(y, 2)].reshape(2 * pitch, channels)
        turned[:, pl.ds(y * pitch, 2 * pitch)] = entry.astype(BF).T
    lay_out((own_ref.shape[0], pitch, tile_cols), own_ref, left_ref, right_ref, taps, wide)
    length = rows * pitch
    for ey in range(3):
        for ex in range(3):
            patch = taps[ex, pl.ds(ey * pitch, length), :]
            product[:, ex * channels : (ex + 1) * channels] = jnp.dot(
                turned[...], patch, preferred_element_type=F32
            )
        at = pl.ds(ey * 3 * channels, 3 * channels)
        spread_rows(where, product, keep.at[:, at], send.at[:, at], layout)
    keep_hbm[0] = keep[...]
    send_hbm[0] = send[...].astype(BF)


def tile_gradient(where, layout, start, received, tall, left, right, extent, pool, downs, acrosses):
    tile_rows, tile_cols, channels = start.shape
    slots, depth, _ = received.shape
    rows, pitch = tile_rows + extent, tile_cols + extent
    smem = pl.BlockSpec(memory_space=pltpu.SMEM)
    vmem = pl.BlockSpec(memory_space=pltpu.VMEM)
    geometry = (slots, extent, pool, tile_rows, tile_cols, downs, acrosses, layout)
    return pl.pallas_call(
        functools.partial(tile_body, geometry),
        in_specs=[smem] + [vmem] * 5,
        out_specs=[vmem, vmem, vmem],
        out_shape=[
            jax.ShapeDtypeStruct((rows, pitch, channels), F32),
            jax.ShapeDtypeStruct((1, channels // 2, 9 * channels), F32),
            jax.ShapeDtypeStruct((1, channels // 2, 9 * channels), BF),
        ],
        scratch_shapes=[
            pltpu.VMEM((3, (rows + 2) * pitch, channels), BF),
            pltpu.VMEM(((rows + 2) * pitch + 16, channels), F32),
            pltpu.VMEM((channels, rows * pitch), BF),
            pltpu.VMEM((channels, 3 * channels), F32),
            pltpu.VMEM((channels // 2, 9 * channels), F32),
            pltpu.VMEM((channels // 2, 9 * channels), F32),
            pltpu.VMEM((slots, extent, ceil_to(depth, 128)), F32),
            pltpu.VMEM((slots, extent + 8, ceil_to(depth, 128)), F32),
            pltpu.VMEM((ceil_to(depth, 128), channels), BF),
            pltpu.VMEM((slots, 128), jnp.int32),
            pltpu.SMEM((slots, 128), jnp.int32),
            pltpu.SemaphoreType.DMA((1,)),
        ],
        compiler_params=params(),
        cost_estimate=cost(36 * rows * pitch * channels * channels),
        name="tile_gradient",
    )(where, start, received, tall, left, right)


def tile_input_body(pitch, rows, left_ref, mid_ref, right_ref, weight, out_ref):
    refs = (left_ref, mid_ref, right_ref)
    half = rows // 2
    for part in range(2):
        total = None
        for ey in range(3):
            for ex in range(3):
                term = lax.dot_general(
                    refs[ex][pl.ds((part * half + ey) * pitch, half * pitch), :],
                    weight[2 - ey, 2 - ex],
                    NT,
                    preferred_element_type=F32,
                )
                total = term if total is None else total + term
        out_ref[pl.ds(part * half * pitch, half * pitch), :] = total.astype(BF)


def tile_input_grad(shifted_grads, weight):
    rows, pitch, channels = shifted_grads[0].shape
    rows = rows - 2
    flat = [a.reshape((rows + 2) * pitch, channels) for a in shifted_grads]
    out = pl.pallas_call(
        functools.partial(tile_input_body, pitch, rows),
        out_shape=jax.ShapeDtypeStruct((rows * pitch, channels), BF),
        compiler_params=params(),
        cost_estimate=cost(),
        name="tile_input_grad",
    )(*flat, weight)
    return out.reshape(rows, pitch, channels)


def neighbours(array, axis, by):
    count = lax.axis_size(axis)
    return lax.ppermute(array, axis, [(i, i + by) for i in range(count) if 0 <= i + by < count])


def partner(array, bits_ty, bits_tx):
    down, across = lax.axis_size("ty"), lax.axis_size("tx")
    if bits_ty == 0:
        return lax.ppermute(array, "tx", [(i, i ^ bits_tx) for i in range(across)])
    if bits_tx == 0:
        return lax.ppermute(array, "ty", [(i, i ^ bits_ty) for i in range(down)])
    pairs = [
        (t * across + s, (t ^ bits_ty) * across + (s ^ bits_tx)) for t in range(down) for s in range(across)
    ]
    return lax.ppermute(array, ("ty", "tx"), pairs)


def sum_pairs(keep, send, layout):
    chips, highs, share = layout
    got = partner(send, 1, 0)
    return (keep + got.astype(F32)).reshape(keep.shape[0], chips * 2, highs * share, keep.shape[2])


def sum_chips(total, layout):
    chips, highs, share = layout
    arrived = [
        partner(total[:, 2 * a + b].astype(BF), 2 * a, b) for a in range(chips) for b in range(2) if a or b
    ]
    total = total[:, 0] + sum(got.astype(F32) for got in arrived)
    return total.reshape(total.shape[0], highs, share, total.shape[2])


def sum_rest(total, layout):
    chips, highs, share = layout
    arrived = [partner(total[:, k].astype(BF), 0, 2 * k) for k in range(1, highs)]
    return (total[:, 0] + sum(got.astype(F32) for got in arrived)).reshape(total.shape[0], -1)


def after(value, *earlier):
    return lax.optimization_barrier((value, earlier))[0]


def local(
    roi_feat,
    pre_one,
    grad_two,
    w_one,
    w_two,
    roi_rows,
    roi_cols,
    target_col,
    off_row,
    off_col,
    fpn_input,
    fpn_grad,
    w_fpn,
):
    regions, pool, channels = roi_feat.shape[0], roi_feat.shape[1], roi_feat.shape[3]
    tile_rows, tile_cols = fpn_input.shape[0], fpn_input.shape[1]
    extent = roi_rows.shape[1]
    down, across = lax.axis_size("ty"), lax.axis_size("tx")
    ty, tx = lax.axis_index("ty"), lax.axis_index("tx")
    capacity = max(2, (2 * regions + across - 1) // across)
    layout = (down // 2, across // 2, channels // (down * across))
    where = jnp.stack([ty, tx]).astype(jnp.int32)

    grad_one, sent = region_heads(
        grad_two, pre_one, w_two, w_one, roi_rows, roi_cols, target_col.reshape(-1), off_row, off_col, across, capacity
    )
    received = lax.all_to_all(sent, "tx", 0, 0, tiled=True)

    terms = head_weight_grads(where, layout, grad_two, pre_one, grad_one, roi_feat)
    heads = sum_pairs(*terms, layout)

    above = neighbours(fpn_input[tile_rows - 1 :], "ty", 1)
    below = neighbours(fpn_input[:extent], "ty", -1)
    tall = jnp.concatenate([above, fpn_input, below], axis=0)
    left = neighbours(tall[:, tile_cols - 1 :], "tx", 1)
    right = neighbours(tall[:, :extent], "tx", -1)

    heads = sum_chips(heads, layout)
    canvas, *terms = tile_gradient(
        where, layout, after(fpn_grad, heads), received, tall, left, right, extent, pool, down, across
    )
    total = sum_pairs(*terms, layout)
    canvas = after(canvas, total)
    total = sum_chips(total, layout)

    spilled = neighbours(canvas[:, tile_cols - 1 : tile_cols + extent - 1].astype(BF), "tx", 1)
    first = neighbours(canvas[:, :1].astype(BF), "tx", -1)
    wide = jnp.pad(canvas[:, : tile_cols + 1], ((0, 0), (1, 0), (0, 0)))
    wide = wide + jnp.pad(spilled.astype(F32), ((0, 0), (0, tile_cols + 2 - extent), (0, 0)))
    wide = wide + jnp.pad(first.astype(F32), ((0, 0), (tile_cols + 1, 0), (0, 0)))
    head_fpn = sum_rest(after(total, wide), layout)
    heads = sum_rest(after(heads, wide), layout)
    spilled = neighbours(wide[tile_rows - 1 : tile_rows + extent - 1].astype(BF), "ty", 1)
    first = neighbours(wide[:1].astype(BF), "ty", -1)
    tall = jnp.pad(wide[: tile_rows + 1], ((1, 0), (0, 0), (0, 0)))
    tall = tall + jnp.pad(spilled.astype(F32), ((0, tile_rows + 2 - extent), (0, 0), (0, 0)))
    tall = (tall + jnp.pad(first.astype(F32), ((tile_rows + 1, 0), (0, 0), (0, 0)))).astype(BF)
    input_grad = tile_input_grad([tall[:, e : e + tile_cols] for e in range(3)], w_fpn)
    return (input_grad, heads[1], heads[0], head_fpn[0])


def solution(mesh):
    placed = (
        P(("ty", "tx"), None, None, None),
        P(("ty", "tx"), None, None, None),
        P(("ty", "tx"), None, None, None),
        P(),
        P(),
        P(("ty", "tx"), None, None),
        P(("ty", "tx"), None, None),
        P(("ty", "tx"), None),
        P(("ty", "tx")),
        P(("ty", "tx")),
        P("ty", "tx", None),
        P("ty", "tx", None),
        P(),
    )
    return jax.shard_map(
        local,
        mesh=mesh,
        in_specs=placed,
        out_specs=(P("ty", "tx", None), P(("ty", "tx")), P(("ty", "tx")), P(("ty", "tx"))),
        check_vma=False,
    )
```

```python
import functools

import jax
import jax.numpy as jnp
from jax import lax
from jax.experimental import pallas as pl
from jax.experimental.pallas import tpu as pltpu
from jax.sharding import PartitionSpec as P

BF = jnp.bfloat16
F32 = jnp.float32
VMEM_BYTES = 56 << 20
NT = (((1,), (1,)), ((), ()))


def ceil_to(value, multiple):
    return -(-value // multiple) * multiple


def slot_rows(pool):
    return ceil_to(pool * pool + 3, 8)


def params():
    return pltpu.CompilerParams(vmem_limit_bytes=VMEM_BYTES)


def cost(flops=1):
    return pl.CostEstimate(flops=int(flops), bytes_accessed=1, transcendentals=0)


def whole(array):
    return pl.BlockSpec(array.shape, lambda *_: (0,) * array.ndim)


def head_body(geometry, target, off_row, off_col, row_ref, col_ref, grad_hbm, pre_hbm, w_two_hbm, w_one_hbm, *rest):
    pool, pitch, regions, capacity, columns, together = geometry
    one_hbm, out = rest[0], rest[1]
    (order, slot_at, held, facts, bare, grads, pres, ones, w_two, w_one, wide, mask, again, packed, taps, sems, out_sems, w_sems) = rest[2:]
    block = (pool + 1) * pitch
    length, rows = together * block + pitch, together * block - pitch

    for j, (src, dst) in enumerate(((w_two_hbm, w_two), (w_one_hbm, w_one))):
        pltpu.make_async_copy(src, dst, w_sems.at[j]).start()
    for q in range(columns):
        held[q] = 0

    def scan(r, count):
        group = target[r]
        rank = held[group]
        held[group] = rank + 1
        order[count] = r
        slot_at[count] = group * capacity + rank
        return count + 1

    count = lax.fori_loop(0, regions, scan, 0)
    steps = (count + together - 1) // together

    def loads(step, which):
        copies = []
        for r in range(together):
            region = order[jnp.minimum(step * together + r, count - 1)]
            for j, (src, dst) in enumerate(((grad_hbm, grads), (pre_hbm, pres))):
                copies.append(pltpu.make_async_copy(src.at[region], dst.at[which, r], sems.at[which, r, j]))
        return copies

    def store(step, which, r):
        region = order[jnp.minimum(step * together + r, count - 1)]
        return pltpu.make_async_copy(
            ones.at[which, pl.ds(r * block, block)],
            one_hbm.at[pl.ds(pl.multiple_of(region * block, block), block)],
            out_sems.at[which, r],
        )

    def settle(step, which):
        for r in range(together):

            @pl.when(step * together + r < count)
            def _(r=r):
                store(step, which, r).wait()

    @pl.when(count > 0)
    def _():
        for copy in loads(0, 0):
            copy.start()

    channels, bins = wide.shape[1], pool * pool
    extent = row_ref.shape[1]
    lane = lax.broadcasted_iota(jnp.int32, (128, channels), 1)
    own = lax.broadcasted_iota(jnp.int32, (128, channels), 0) == lane % pool
    spread = jnp.where(own & (lane < extent * pool), 1.0, 0.0).astype(BF)
    flat = (regions * extent, channels)
    own = lax.broadcasted_iota(jnp.int32, flat, 0) % extent == lax.broadcasted_iota(jnp.int32, flat, 1) // pool
    bare[...] = jnp.zeros_like(bare)
    for j, ref in enumerate((row_ref, col_ref)):
        bare[:, pl.ds(0, pool)] = ref[...].reshape(regions * extent, pool).astype(F32)
        entry = jnp.dot(bare[...].astype(BF), spread, preferred_element_type=F32)
        entry = jnp.where(own, entry, 0.0).reshape(regions, extent, channels)
        facts[j, pl.ds(0, regions), :] = jnp.sum(entry, axis=1)
    lane = lax.broadcasted_iota(jnp.int32, (1, channels), 1)
    out[...] = jnp.zeros_like(out)
    wide[...] = jnp.zeros_like(wide)
    again[...] = jnp.zeros_like(again)
    mask[...] = jnp.zeros_like(mask)
    packed[...] = jnp.zeros_like(packed)
    for which in range(2):
        for r in range(together):
            ones[which, pl.ds((r + 1) * block - pitch, pitch), :] = jnp.zeros((pitch, wide.shape[1]), BF)
    pltpu.make_async_copy(w_two_hbm, w_two, w_sems.at[0]).wait()

    def conv(source, weight):
        for e in range(3):
            taps[e] = source[pl.ds(7 + e, length), :].astype(BF)
        total = None
        for ey in range(3):
            for ex in range(3):
                term = lax.dot_general(
                    taps[ex, pl.ds(ey * pitch, rows), :],
                    weight[2 - ey, 2 - ex],
                    NT,
                    preferred_element_type=F32,
                )
                total = term if total is None else total + term
        return total

    def turn(step, carry):
        which = step % 2

        @pl.when(step + 1 < steps)
        def _():
            for copy in loads(step + 1, 1 - which):
                copy.start()

        for copy in loads(step, which):
            copy.wait()

        @pl.when(step >= 2)
        def _():
            settle(step - 2, which)

        for r in range(together):
            for y in range(pool):
                at = r * block + y * pitch
                wide[pl.ds(8 + pitch + at, pool), :] = grads[which, r, y].astype(F32)
                mask[pl.ds(at, pool), :] = pres[which, r, y].astype(F32)
        grad_one = jnp.where(mask[pl.ds(0, rows), :] > 0, conv(wide, w_two), 0.0)
        again[pl.ds(8 + pitch, rows), :] = grad_one
        ones[which, pl.ds(0, rows), :] = grad_one.astype(BF)
        for r in range(together):

            @pl.when(step * together + r < count)
            def _(r=r):
                store(step, which, r).start()

        @pl.when(step == 0)
        def _():
            pltpu.make_async_copy(w_one_hbm, w_one, w_sems.at[1]).wait()

        region_grad = conv(again, w_one)
        for r in range(together):
            for y in range(pool):
                at = r * block + y * pitch
                packed[pl.ds(y * pool, pitch), :] = region_grad[at : at + pitch]
            at = jnp.minimum(step * together + r, count - 1)
            region = order[at]
            for j in range(2):
                packed[pl.ds(bins + j, 1), :] = facts[j, pl.ds(region, 1), :]
            place = jnp.where(lane == 0, off_row[region], jnp.where(lane == 1, off_col[region], lane == 2))
            packed[pl.ds(bins + 2, 1), :] = place.astype(F32)
            out[slot_at[at]] = packed[pl.ds(0, out.shape[1]), :].astype(BF)

        return carry

    lax.fori_loop(0, steps, turn, 0)

    @pl.when(steps > 1)
    def _():
        settle(steps - 2, steps % 2)

    @pl.when(steps > 0)
    def _():
        settle(steps - 1, (steps - 1) % 2)


def region_heads(grad_two, pre_one, w_two, w_one, roi_rows, roi_cols, target, off_row, off_col, columns, capacity, together=2):
    regions, pool, _, channels = grad_two.shape
    pitch = ceil_to(pool + 1, 16)
    block = (pool + 1) * pitch
    length = together * block + pitch
    anywhere = pl.BlockSpec(memory_space=pl.ANY)
    smem = pl.BlockSpec(memory_space=pltpu.SMEM)
    vmem = pl.BlockSpec(memory_space=pltpu.VMEM)
    return pl.pallas_call(
        functools.partial(head_body, (pool, pitch, regions, capacity, columns, together)),
        in_specs=[smem] * 3 + [vmem] * 2 + [anywhere] * 4,
        out_specs=[anywhere, vmem],
        out_shape=[
            jax.ShapeDtypeStruct((regions * block, channels), BF),
            jax.ShapeDtypeStruct((columns * capacity, slot_rows(pool), channels), BF),
        ],
        scratch_shapes=[
            pltpu.SMEM((regions,), jnp.int32),
            pltpu.SMEM((regions,), jnp.int32),
            pltpu.SMEM((columns,), jnp.int32),
            pltpu.VMEM((2, ceil_to(regions, 8), channels), F32),
            pltpu.VMEM((regions * roi_rows.shape[1], 128), F32),
            pltpu.VMEM((2, together, pool, pool, channels), BF),
            pltpu.VMEM((2, together, pool, pool, channels), BF),
            pltpu.VMEM((2, together * block, channels), BF),
            pltpu.VMEM(w_two.shape, BF),
            pltpu.VMEM(w_one.shape, BF),
            pltpu.VMEM((length + 16, channels), F32),
            pltpu.VMEM((length, channels), F32),
            pltpu.VMEM((length + 16, channels), F32),
            pltpu.VMEM((pool * pool + pitch, channels), F32),
            pltpu.VMEM((3, length, channels), BF),
            pltpu.SemaphoreType.DMA((2, together, 2)),
            pltpu.SemaphoreType.DMA((2, together)),
            pltpu.SemaphoreType.DMA((2,)),
        ],
        compiler_params=params(),
        cost_estimate=cost(72 * regions * block * channels * channels),
        name="region_heads",
    )(target, off_row, off_col, roi_rows, roi_cols, grad_two, pre_one, w_two, w_one)


def spread_rows(where, source, keep, send, layout):
    chips, highs, share = layout
    core, chip, low, high = where[0] % 2, where[0] // 2, where[1] % 2, where[1] // 2
    for other, out in enumerate((keep, send)):
        for a in range(chips):
            for b in range(2):
                for k in range(highs):
                    block = (((chip ^ a) * 2 + (core ^ other)) * highs + (high ^ k)) * 2 + (low ^ b)
                    place = ((a * 2 + b) * highs + k) * share
                    if share % 8 == 0:
                        rows = source[pl.ds(pl.multiple_of(block * share, 8), share), :]
                    else:
                        rows = source[pl.ds(pl.multiple_of(block * share // 8 * 8, 8), 8), :]
                        rows = pltpu.roll(rows, (8 - block * share % 8) % 8, 0)[:share]
                    out[pl.ds(place, share), :] = rows


def head_weight_body(geometry, where, two_ref, pre_ref, one_hbm, feat_hbm, keep_ref, send_ref, one, feat, turned, wide, taps, product, passed, sems):
    regions, pool, pitch, layout = geometry
    block = (pool + 1) * pitch
    length = turned.shape[1]
    step = pl.program_id(0)
    copies = [pltpu.make_async_copy(one_hbm, one, sems.at[0]), pltpu.make_async_copy(feat_hbm, feat, sems.at[1])]

    def lay_out(ref, relu):
        for r in range(regions):
            for y in range(pool):
                entry = ref[r, y].astype(F32)
                wide[pl.ds(8 + pitch + r * block + y * pitch, pool), :] = jnp.maximum(entry, 0.0) if relu else entry
        for e in range(3):
            taps[e] = wide[pl.ds(7 + e, length + 2 * pitch), :].astype(BF)

    @pl.when(step == 0)
    def _():
        for copy in copies:
            copy.start()
        wide[...] = jnp.zeros_like(wide)
        turned[...] = jnp.zeros_like(turned)
        lay_out(two_ref, False)
        for r in range(regions):
            turned[:, pl.ds(r * block, block)] = taps[1, pl.ds(pitch + r * block, block), :].T
        lay_out(pre_ref, True)

    @pl.when(step == 3)
    def _():
        for copy in copies:
            copy.wait()
        for r in range(regions):
            turned[:, pl.ds(r * block, block)] = one[pl.ds(r * block, block), :].T
        lay_out(feat, False)

    channels = taps.shape[2]
    for ex in range(3):
        patch = taps[ex, pl.ds(pl.multiple_of(step % 3 * pitch, pitch), length), :]
        product[:, ex * channels : (ex + 1) * channels] = jnp.dot(turned[...], patch, preferred_element_type=F32)
    spread_rows(where, product, keep_ref.at[0], passed, layout)
    send_ref[0] = passed[...].astype(BF)


def head_weight_grads(where, layout, grad_two, pre_one, grad_one, roi_feat):
    regions, pool, _, channels = roi_feat.shape
    pitch = ceil_to(pool + 1, 16)
    length = ceil_to(regions * (pool + 1) * pitch, 128)
    anywhere = pl.BlockSpec(memory_space=pl.ANY)
    out = pl.BlockSpec((1, channels // 2, 3 * channels), lambda s: (s // 3, 0, s % 3))
    return pl.pallas_call(
        functools.partial(head_weight_body, (regions, pool, pitch, layout)),
        grid=(6,),
        in_specs=[pl.BlockSpec(memory_space=pltpu.SMEM), whole(grad_two), whole(pre_one), anywhere, anywhere],
        out_specs=[out, out],
        out_shape=[
            jax.ShapeDtypeStruct((2, channels // 2, 9 * channels), F32),
            jax.ShapeDtypeStruct((2, channels // 2, 9 * channels), BF),
        ],
        scratch_shapes=[
            pltpu.VMEM(grad_one.shape, BF),
            pltpu.VMEM(roi_feat.shape, BF),
            pltpu.VMEM((channels, length), BF),
            pltpu.VMEM((length + 2 * pitch + 16, channels), F32),
            pltpu.VMEM((3, length + 2 * pitch, channels), BF),
            pltpu.VMEM((channels, 3 * channels), F32),
            pltpu.VMEM((channels // 2, 3 * channels), F32),
            pltpu.SemaphoreType.DMA((2,)),
        ],
        compiler_params=params(),
        cost_estimate=cost(),
        name="head_weight_grads",
    )(where, grad_two, pre_one, grad_one, roi_feat)


def lay_out(geometry, own_ref, left_ref, right_ref, out_ref, wide):
    rows, pitch, tile_cols = geometry
    end = 8 + rows * pitch
    wide[pl.ds(0, 8), :] = jnp.zeros((8, wide.shape[1]), F32)
    wide[pl.ds(end, wide.shape[0] - end), :] = jnp.zeros((wide.shape[0] - end, wide.shape[1]), F32)
    for y in range(rows):
        at = 8 + y * pitch
        wide[pl.ds(at, tile_cols), :] = own_ref[y].astype(F32)
        wide[pl.ds(at + tile_cols, pitch - tile_cols), :] = right_ref[y].astype(F32)
    for e in (1, 2):
        out_ref[e] = wide[pl.ds(7 + e, out_ref.shape[1]), :].astype(BF)
    for y in range(rows):
        wide[pl.ds(7 + y * pitch, 1), :] = left_ref[y].astype(F32)
    out_ref[0] = wide[pl.ds(7, out_ref.shape[1]), :].astype(BF)


def place_all(geometry, received, start_ref, canvas, row_spread, col_spread, block, numbers, place, sem):
    slots, extent, pool, tile_rows, tile_cols = geometry
    depth, channels = received.shape[1], received.shape[2]
    wide, bins = extent + 8, pool * pool
    facts = received[:, pl.ds(bins // 8 * 8, depth - bins // 8 * 8), :].astype(F32)
    numbers[...] = facts[:, bins % 8 + 2, :128].astype(jnp.int32)
    copy = pltpu.make_async_copy(numbers, place, sem)
    copy.start()
    full = block.shape[0]
    lane = lax.broadcasted_iota(jnp.int32, (channels, full), 1)
    source = lax.broadcasted_iota(jnp.int32, (channels, full), 0) % pool
    own = lax.broadcasted_iota(jnp.int32, (slots, extent, channels), 1) == (
        lax.broadcasted_iota(jnp.int32, (slots, extent, channels), 2) // pool
    )
    for j, (out, part) in enumerate(((row_spread, lane // pool), (col_spread, lane % pool))):
        chosen = jnp.where((part == source) & (lane < bins), 1.0, 0.0).astype(BF)
        entry = jnp.broadcast_to(facts[:, bins % 8 + j : bins % 8 + j + 1, :], (slots, extent, channels))
        entry = jnp.where(own, entry, 0.0).astype(BF).reshape(slots * extent, channels)
        entry = jnp.dot(entry, chosen, preferred_element_type=F32).reshape(slots, extent, full)
        out[:, pl.ds(0, extent), :] = entry
    col_spread[:, pl.ds(extent, 8), :] = jnp.zeros((slots, 8, full), F32)
    block[...] = jnp.zeros_like(block)
    canvas[...] = jnp.zeros_like(canvas)
    canvas[pl.ds(0, tile_rows), pl.ds(0, tile_cols), :] = start_ref[...].astype(F32)
    copy.wait()

    def put(slot, carry):
        @pl.when(place[slot, 2] > 0)
        def _():
            row, col = place[slot, 0], place[slot, 1]
            cols = pltpu.roll(col_spread[slot], col % 8, 0)
            rows = row_spread[slot]
            weights = jnp.concatenate([rows[y : y + 1] * cols for y in range(extent)], axis=0).astype(BF)
            block[pl.ds(0, depth), :] = received[slot]
            window = jnp.dot(weights, block[...], preferred_element_type=F32)
            at = pl.multiple_of(col // 8 * 8, 8)
            for y in range(extent):
                here = (row + y, pl.ds(at, wide))
                canvas[here] = canvas[here] + window[y * wide : (y + 1) * wide]

        return carry

    lax.fori_loop(0, slots, put, 0)


def tile_body(geometry, where, start_ref, received, own_ref, left_ref, right_ref, canvas, keep_hbm, send_hbm, taps, wide, turned, product, keep, send, row_spread, col_spread, block, numbers, place, sems):
    slots, extent, pool, tile_rows, tile_cols, downs, acrosses, layout = geometry
    rows, pitch, channels = canvas.shape
    place_all(
        (slots, extent, pool, tile_rows, tile_cols), received, start_ref, canvas, row_spread, col_spread, block, numbers, place, sems.at[0]
    )

    @pl.when(where[0] == downs - 1)
    def _():
        canvas[pl.ds(tile_rows, extent)] = jnp.zeros((extent, pitch, channels), F32)

    @pl.when(where[1] == acrosses - 1)
    def _():
        canvas[:, pl.ds(tile_cols, extent), :] = jnp.zeros((rows, extent, channels), F32)

    for y in range(0, rows, 2):
        entry = canvas[pl.ds(y, 2)].reshape(2 * pitch, channels)
        turned[:, pl.ds(y * pitch, 2 * pitch)] = entry.astype(BF).T
    lay_out((own_ref.shape[0], pitch, tile_cols), own_ref, left_ref, right_ref, taps, wide)
    length = rows * pitch
    for ey in range(3):
        for ex in range(3):
            patch = taps[ex, pl.ds(ey * pitch, length), :]
            product[:, ex * channels : (ex + 1) * channels] = jnp.dot(
                turned[...], patch, preferred_element_type=F32
            )
        at = pl.ds(ey * 3 * channels, 3 * channels)
        spread_rows(where, product, keep.at[:, at], send.at[:, at], layout)
    keep_hbm[0] = keep[...]
    send_hbm[0] = send[...].astype(BF)


def tile_gradient(where, layout, start, received, tall, left, right, extent, pool, downs, acrosses):
    tile_rows, tile_cols, channels = start.shape
    slots, depth, _ = received.shape
    rows, pitch = tile_rows + extent, tile_cols + extent
    smem = pl.BlockSpec(memory_space=pltpu.SMEM)
    vmem = pl.BlockSpec(memory_space=pltpu.VMEM)
    geometry = (slots, extent, pool, tile_rows, tile_cols, downs, acrosses, layout)
    return pl.pallas_call(
        functools.partial(tile_body, geometry),
        in_specs=[smem] + [vmem] * 5,
        out_specs=[vmem, vmem, vmem],
        out_shape=[
            jax.ShapeDtypeStruct((rows, pitch, channels), F32),
            jax.ShapeDtypeStruct((1, channels // 2, 9 * channels), F32),
            jax.ShapeDtypeStruct((1, channels // 2, 9 * channels), BF),
        ],
        scratch_shapes=[
            pltpu.VMEM((3, (rows + 2) * pitch, channels), BF),
            pltpu.VMEM(((rows + 2) * pitch + 16, channels), F32),
            pltpu.VMEM((channels, rows * pitch), BF),
            pltpu.VMEM((channels, 3 * channels), F32),
            pltpu.VMEM((channels // 2, 9 * channels), F32),
            pltpu.VMEM((channels // 2, 9 * channels), F32),
            pltpu.VMEM((slots, extent, ceil_to(depth, 128)), F32),
            pltpu.VMEM((slots, extent + 8, ceil_to(depth, 128)), F32),
            pltpu.VMEM((ceil_to(depth, 128), channels), BF),
            pltpu.VMEM((slots, 128), jnp.int32),
            pltpu.SMEM((slots, 128), jnp.int32),
            pltpu.SemaphoreType.DMA((1,)),
        ],
        compiler_params=params(),
        cost_estimate=cost(36 * rows * pitch * channels * channels),
        name="tile_gradient",
    )(where, start, received, tall, left, right)


def tile_input_body(pitch, rows, left_ref, mid_ref, right_ref, weight, out_ref):
    refs = (left_ref, mid_ref, right_ref)
    half = rows // 2
    for part in range(2):
        total = None
        for ey in range(3):
            for ex in range(3):
                term = lax.dot_general(
                    refs[ex][pl.ds((part * half + ey) * pitch, half * pitch), :],
                    weight[2 - ey, 2 - ex],
                    NT,
                    preferred_element_type=F32,
                )
                total = term if total is None else total + term
        out_ref[pl.ds(part * half * pitch, half * pitch), :] = total.astype(BF)


def tile_input_grad(shifted_grads, weight):
    rows, pitch, channels = shifted_grads[0].shape
    rows = rows - 2
    flat = [a.reshape((rows + 2) * pitch, channels) for a in shifted_grads]
    out = pl.pallas_call(
        functools.partial(tile_input_body, pitch, rows),
        out_shape=jax.ShapeDtypeStruct((rows * pitch, channels), BF),
        compiler_params=params(),
        cost_estimate=cost(),
        name="tile_input_grad",
    )(*flat, weight)
    return out.reshape(rows, pitch, channels)


def neighbours(array, axis, by):
    count = lax.axis_size(axis)
    return lax.ppermute(array, axis, [(i, i + by) for i in range(count) if 0 <= i + by < count])


def partner(array, bits_ty, bits_tx):
    down, across = lax.axis_size("ty"), lax.axis_size("tx")
    if bits_ty == 0:
        return lax.ppermute(array, "tx", [(i, i ^ bits_tx) for i in range(across)])
    if bits_tx == 0:
        return lax.ppermute(array, "ty", [(i, i ^ bits_ty) for i in range(down)])
    pairs = [
        (t * across + s, (t ^ bits_ty) * across + (s ^ bits_tx)) for t in range(down) for s in range(across)
    ]
    return lax.ppermute(array, ("ty", "tx"), pairs)


def sum_pairs(keep, send, layout):
    chips, highs, share = layout
    got = partner(send, 1, 0)
    return (keep + got.astype(F32)).reshape(keep.shape[0], chips * 2, highs * share, keep.shape[2])


def sum_chips(total, layout):
    chips, highs, share = layout
    arrived = [
        partner(total[:, 2 * a + b].astype(BF), 2 * a, b) for a in range(chips) for b in range(2) if a or b
    ]
    total = total[:, 0] + sum(got.astype(F32) for got in arrived)
    return total.reshape(total.shape[0], highs, share, total.shape[2])


def sum_rest(total, layout):
    chips, highs, share = layout
    arrived = [partner(total[:, k].astype(BF), 0, 2 * k) for k in range(1, highs)]
    return (total[:, 0] + sum(got.astype(F32) for got in arrived)).reshape(total.shape[0], -1)


def after(value, *earlier):
    return lax.optimization_barrier((value, earlier))[0]


def local(
    roi_feat,
    pre_one,
    grad_two,
    w_one,
    w_two,
    roi_rows,
    roi_cols,
    target_col,
    off_row,
    off_col,
    fpn_input,
    fpn_grad,
    w_fpn,
):
    regions, pool, channels = roi_feat.shape[0], roi_feat.shape[1], roi_feat.shape[3]
    tile_rows, tile_cols = fpn_input.shape[0], fpn_input.shape[1]
    extent = roi_rows.shape[1]
    down, across = lax.axis_size("ty"), lax.axis_size("tx")
    ty, tx = lax.axis_index("ty"), lax.axis_index("tx")
    capacity = max(2, (2 * regions + across - 1) // across)
    layout = (down // 2, across // 2, channels // (down * across))
    where = jnp.stack([ty, tx]).astype(jnp.int32)

    grad_one, sent = region_heads(
        grad_two, pre_one, w_two, w_one, roi_rows, roi_cols, target_col.reshape(-1), off_row, off_col, across, capacity
    )
    received = lax.all_to_all(sent, "tx", 0, 0, tiled=True)

    terms = head_weight_grads(where, layout, grad_two, pre_one, grad_one, roi_feat)
    heads = sum_pairs(*terms, layout)

    above = neighbours(fpn_input[tile_rows - 1 :], "ty", 1)
    below = neighbours(fpn_input[:extent], "ty", -1)
    tall = jnp.concatenate([above, fpn_input, below], axis=0)
    left = neighbours(tall[:, tile_cols - 1 :], "tx", 1)
    right = neighbours(tall[:, :extent], "tx", -1)

    heads = sum_chips(heads, layout)
    canvas, *terms = tile_gradient(
        where, layout, after(fpn_grad, heads), received, tall, left, right, extent, pool, down, across
    )
    total = sum_pairs(*terms, layout)
    canvas = after(canvas, total)
    total = sum_chips(total, layout)

    spilled = neighbours(canvas[:, tile_cols - 1 : tile_cols + extent - 1].astype(BF), "tx", 1)
    first = neighbours(canvas[:, :1].astype(BF), "tx", -1)
    wide = jnp.pad(canvas[:, : tile_cols + 1], ((0, 0), (1, 0), (0, 0)))
    wide = wide + jnp.pad(spilled.astype(F32), ((0, 0), (0, tile_cols + 2 - extent), (0, 0)))
    wide = wide + jnp.pad(first.astype(F32), ((0, 0), (tile_cols + 1, 0), (0, 0)))
    head_fpn = sum_rest(after(total, wide), layout)
    heads = sum_rest(after(heads, wide), layout)
    spilled = neighbours(wide[tile_rows - 1 : tile_rows + extent - 1].astype(BF), "ty", 1)
    first = neighbours(wide[:1].astype(BF), "ty", -1)
    tall = jnp.pad(wide[: tile_rows + 1], ((1, 0), (0, 0), (0, 0)))
    tall = tall + jnp.pad(spilled.astype(F32), ((0, tile_rows + 2 - extent), (0, 0), (0, 0)))
    tall = (tall + jnp.pad(first.astype(F32), ((tile_rows + 1, 0), (0, 0), (0, 0)))).astype(BF)
    input_grad = tile_input_grad([tall[:, e : e + tile_cols] for e in range(3)], w_fpn)
    return (input_grad, heads[1], heads[0], head_fpn[0])


def solution(mesh):
    placed = (
        P(("ty", "tx"), None, None, None),
        P(("ty", "tx"), None, None, None),
        P(("ty", "tx"), None, None, None),
        P(),
        P(),
        P(("ty", "tx"), None, None),
        P(("ty", "tx"), None, None),
        P(("ty", "tx"), None),
        P(("ty", "tx")),
        P(("ty", "tx")),
        P("ty", "tx", None),
        P("ty", "tx", None),
        P(),
    )
    return jax.shard_map(
        local,
        mesh=mesh,
        in_specs=placed,
        out_specs=(P("ty", "tx", None), P(("ty", "tx")), P(("ty", "tx")), P(("ty", "tx"))),
        check_vma=False,
    )
```
